256 devices in a mesh: leaf: 32 (over z, x), blk: 8 (over y, core).
Axes of the slice: x: 4, y: 4, z: 8, core: 2. Of those that a mesh axis runs over, the one named last changes fastest.
Arguments:
- rhs: float32 [6, 32, 4096], P(None, None, ('leaf', 'blk')), may hold values from -6 to 6
- diag_inverse: float32 [4096, 8064], P(('leaf', 'blk')), as said below
- off_diagonal: float32 [5, 4096, 512], P(None, ('leaf', 'blk')), may hold values from -0.1875 to 0.1875
- rows_index: int32 [5, 256, 512], P(None, ('leaf', 'blk')), may hold values from 0 to 7935, as said below
Outputs:
- solution: float32 [6, 32, 4096], P(None, None, ('leaf', 'blk'))
The draws below stay inside these ranges and needn't reach their ends.
Inputs may be any that keep to these rules, and one draw needn't show every extreme that they name: `diag_inverse`: each level's packed block is lower triangular with a positive diagonal; entries to the right of a supernode's width within its level are zero. `rows_index`: an entry of level l lies below (2**6 - 2**(l+1)) * 128.
All inputs are finite; a program needn't handle non-finite values.
Results may differ from the reference program's by a relative error of at most 0.00013.
Values sent between devices are 32-bit elements; how exact they have to be, the bound alone decides.
No kernel may reach another device: no remote copies, remote signals or barrier semaphores. Data moves between devices by JAX's collectives and lax.ppermute only.
A program may use at most 64 MiB of HBM per device.

```python
import jax
import jax.numpy as jnp
from jax import lax

NRHS = 32
B = 16
R = 512
LEVELS = 6
UNIT = 128
LEVEL_ROWS = 4096
CHAIN_ROWS = 8064
N_BLK = 8
DEVICES = 256


def draw_diag_inverse(key, part):
    key = jax.random.fold_in(key, 5)
    first, second = jax.random.split(key)
    rows_here = jnp.arange(LEVEL_ROWS, dtype=jnp.int32)[:, None]
    columns = jnp.arange(CHAIN_ROWS, dtype=jnp.int32)[None, :]
    ancestor = jnp.zeros_like(columns)
    for step in range(1, LEVELS):
        ancestor = ancestor + (columns >= (2 ** step - 1) * UNIT).astype(jnp.int32)
    breadth = jnp.power(2, ancestor).astype(jnp.int32) * UNIT
    inner = columns - (breadth - UNIT)
    within = rows_here % breadth
    scaling = 0.6 / jnp.sqrt(breadth.astype(jnp.float32))
    noise = jnp.clip(jax.random.normal(first, (LEVEL_ROWS, CHAIN_ROWS), jnp.float32), -6.0, 6.0) * scaling
    diagonal = jax.random.uniform(second, (LEVEL_ROWS, CHAIN_ROWS), jnp.float32, 0.6, 1.4)
    return jnp.where(inner < within, noise, jnp.where(inner == within, diagonal, 0.0)).astype(jnp.float32)


def draw_rows_index(key, part):
    key = jax.random.fold_in(key, 11)
    first, second, third = jax.random.split(key, 3)
    heights = jnp.arange(LEVELS - 1, dtype=jnp.int32)[:, None, None]
    ceiling = (2 ** LEVELS - jnp.power(2, heights + 1).astype(jnp.int32)) * UNIT
    values = jax.random.randint(first, (LEVELS - 1, DEVICES, R), 0, ceiling, dtype=jnp.int32)
    device_pick = jax.random.randint(second, (), 0, DEVICES, dtype=jnp.int32)
    slot_pick = jax.random.randint(third, (), 0, R, dtype=jnp.int32)
    values = values.at[0, device_pick, slot_pick].set((2 ** LEVELS - 2) * UNIT - 1)
    return values.astype(jnp.int32)


def block_levels(key, dims, shards, smallest, top_value):
    def one(dim, parts):
        steps = jax.random.uniform(jax.random.fold_in(jax.random.fold_in(key, 6), dim), (parts,), jnp.float32, smallest / len(shards), top_value / len(shards))
        return jnp.repeat(jnp.exp(steps), dims[dim] // parts).reshape((-1,) + (1,) * (len(dims) - dim - 1))

    loudness = one(*shards[0])
    for cut in shards[1:]:
        loudness = loudness * one(*cut)
    return loudness


def gaussian(key, extent, width, most, cuts=(), kind=jnp.bfloat16):
    drawn = jax.random.normal(key, extent, jnp.float32) * width
    if len(cuts) > 0:
        drawn = block_levels(key, extent, cuts, -0.22, 0.18) * drawn
    return jnp.clip(drawn, min=-most, max=most).astype(kind)


def setup_inputs(seed: int = 0) -> dict:
    key_of = jax.random.split(jax.random.key(seed), 5)
    rhs = gaussian(key_of[0], (LEVELS, NRHS, LEVEL_ROWS), 1.0, 6.0, ((2, 256),), jnp.float32)
    diag_inverse = draw_diag_inverse(jax.random.fold_in(key_of[4], 71), 0)
    off_diagonal = gaussian(key_of[2], (LEVELS - 1, LEVEL_ROWS, R), (2 * R) ** -0.5, 0.1875, ((1, 256),), jnp.float32)
    rows_index = draw_rows_index(jax.random.fold_in(key_of[4], 71), 0)
    return dict(rhs=rhs, diag_inverse=diag_inverse, off_diagonal=off_diagonal, rows_index=rows_index)


def chain_targets(index_rows, height):
    devices = jnp.arange(DEVICES, dtype=jnp.int32)[:, None]
    leaf_group = devices // N_BLK
    position = (2 ** (height + 1) - 1) * UNIT + index_rows.astype(jnp.int32)
    ancestor = jnp.zeros_like(position)
    for step in range(1, LEVELS):
        ancestor = ancestor + (position >= (2 ** step - 1) * UNIT).astype(jnp.int32)
    breadth = jnp.power(2, ancestor).astype(jnp.int32) * UNIT
    base = breadth - UNIT
    owner = jnp.right_shift(leaf_group, ancestor)
    return (ancestor * LEVEL_ROWS + owner * breadth + (position - base)).astype(jnp.int32)


def reference(rhs, diag_inverse, off_diagonal, rows_index):
    highest = lax.Precision.HIGHEST
    residual = jnp.transpose(rhs, (1, 0, 2)).reshape(NRHS, LEVELS * LEVEL_ROWS)
    forward = []
    for height in range(LEVELS):
        breadth = 2 ** height * UNIT
        offset = (2 ** height - 1) * UNIT
        groups = LEVEL_ROWS // breadth
        current = residual[:, height * LEVEL_ROWS:(height + 1) * LEVEL_ROWS].reshape(NRHS, groups, breadth)
        blocks = diag_inverse[:, offset:offset + breadth].reshape(groups, breadth, breadth)
        solved = jnp.einsum('nsw,svw->nsv', current, blocks, precision=highest).reshape(NRHS, LEVEL_ROWS)
        forward.append(solved)
        if height < LEVELS - 1:
            pieces = solved.reshape(NRHS, DEVICES, B)
            factor = off_diagonal[height].reshape(DEVICES, B, R)
            update = jnp.einsum('ndb,dbr->ndr', pieces, factor, precision=highest)
            targets = chain_targets(rows_index[height], height).reshape(-1)
            residual = residual.at[:, targets].add(-update.reshape(NRHS, DEVICES * R))
    answer = jnp.zeros((NRHS, LEVELS * LEVEL_ROWS), jnp.float32)
    for height in reversed(range(LEVELS)):
        breadth = 2 ** height * UNIT
        offset = (2 ** height - 1) * UNIT
        groups = LEVEL_ROWS // breadth
        current = forward[height]
        if height < LEVELS - 1:
            targets = chain_targets(rows_index[height], height).reshape(-1)
            known = answer[:, targets].reshape(NRHS, DEVICES, R)
            factor = off_diagonal[height].reshape(DEVICES, B, R)
            coupling = jnp.einsum('ndr,dbr->ndb', known, factor, precision=highest)
            current = current - coupling.reshape(NRHS, LEVEL_ROWS)
        blocks = diag_inverse[:, offset:offset + breadth].reshape(groups, breadth, breadth)
        solved = jnp.einsum('nsv,svw->nsw', current.reshape(NRHS, groups, breadth), blocks, precision=highest)
        answer = answer.at[:, height * LEVEL_ROWS:(height + 1) * LEVEL_ROWS].set(solved.reshape(NRHS, LEVEL_ROWS))
    return jnp.transpose(answer.reshape(NRHS, LEVELS, LEVEL_ROWS), (1, 0, 2))
```

```python
import functools

import jax
import jax.numpy as jnp
from jax import lax
from jax.experimental import pallas as pl
from jax.experimental.pallas import tpu as pltpu
from jax.sharding import Mesh
from jax.sharding import PartitionSpec as P

PLANE = ("x", "blk")
LANES = 128
BLOCK = 16
BLOCKS = 32
ROWS = BLOCK * BLOCKS
REACH = 512
FIRST = (0, 8, 12, 16, 24, 40)
COUNT = (4, 4, 4, 8, 16, 32)
SPACE = 72
DIAG_AT = (0, 128, 384, 2688, 4224, 6784)
OFF_AT = (896, 1408, 1920, 3712, 6272)
AUX_AT = 2432
VMEM_LIMIT = 40 * 1024 * 1024


def pack_local(diag_inverse, off_diagonal, rows_index):
    named = rows_index[:, 0, :].astype(jnp.float32)
    aux = jnp.pad(named, ((0, 3), (0, 0))).reshape(BLOCK, 256)
    return jnp.concatenate(
        [
            diag_inverse[:, 0:896],
            off_diagonal[0],
            off_diagonal[1],
            off_diagonal[2],
            aux,
            diag_inverse[:, 896:1920],
            off_diagonal[3],
            diag_inverse[:, 1920:3968],
            off_diagonal[4],
            diag_inverse[:, 3968:8064],
        ],
        axis=1,
    )


def matvec(diag, at, groups, chunks, read_row, write):
    size = ROWS // groups
    for k in range(groups):
        for start in range(k * size, (k + 1) * size, 64):
            total = None
            for c in range(chunks):
                term = diag[start : start + 64, at + c * LANES : at + (c + 1) * LANES] * read_row(k * chunks + c)
                total = term if total is None else total + term
            write(start, jnp.sum(total, axis=1, keepdims=True))


def matvec_transposed(diag, at, groups, chunks, wide, write):
    size = ROWS // groups
    for k in range(groups):
        for c in range(chunks):
            total = None
            for start in range(k * size, (k + 1) * size, 64):
                term = diag[start : start + 64, at + c * LANES : at + (c + 1) * LANES] * wide[start : start + 64, :]
                total = term if total is None else total + term
            write(k * chunks + c, jnp.sum(total, axis=0, keepdims=True))


def scatter_update(off, at, wide, place, first, height):
    row_iota = lax.broadcasted_iota(jnp.int32, (height, REACH), 0) + first
    lane_iota = lax.broadcasted_iota(jnp.int32, (LANES, REACH), 0)

    def step(d, total):
        rows = off[pl.ds(pl.multiple_of(d * BLOCK, BLOCK), BLOCK), at : at + REACH]
        solved = wide[pl.ds(pl.multiple_of(d * BLOCK, BLOCK), BLOCK), :]
        solved = jnp.concatenate([solved] * (REACH // LANES), axis=1)
        update = jnp.sum(rows * solved, axis=0, keepdims=True)
        where = place[pl.ds(d, 1), :]
        high = jnp.right_shift(where, 7)
        low = jnp.bitwise_and(where, 127)
        coarse = update.astype(jnp.bfloat16).astype(jnp.float32)
        fine = update - coarse
        hit = row_iota == high
        left = jnp.concatenate(
            [
                jnp.where(hit, coarse, 0.0).astype(jnp.bfloat16),
                jnp.where(hit, fine, 0.0).astype(jnp.bfloat16),
            ],
            axis=0,
        )
        right = jnp.where(lane_iota == low, 1.0, 0.0).astype(jnp.bfloat16)
        return total + lax.dot_general(
            left, right, (((1,), (1,)), ((), ())), preferred_element_type=jnp.float32
        )

    total = lax.fori_loop(0, BLOCKS, step, jnp.zeros((2 * height, LANES), jnp.float32), unroll=4)
    return total[:height] + total[height:]


def gather_known(known, chain, place, first):
    tiles = [(i, j) for i in range(BLOCKS // 8) for j in range(REACH // LANES)]
    cut = [place[i * 8 : (i + 1) * 8, j * LANES : (j + 1) * LANES] for i, j in tiles]
    high = [jnp.right_shift(t, 7) for t in cut]
    low = [jnp.bitwise_and(t, 127) for t in cut]

    def step(h, values):
        row = jnp.broadcast_to(chain[pl.ds(h, 1), :], (8, LANES))
        return tuple(
            jnp.where(
                hi == h,
                jnp.take_along_axis(row, lo, axis=1, mode="promise_in_bounds"),
                v,
            )
            for hi, lo, v in zip(high, low, values)
        )

    zero = jnp.zeros((8, LANES), jnp.float32)
    values = lax.fori_loop(first, SPACE, step, tuple(zero for _ in tiles))
    for (i, j), v in zip(tiles, values):
        known[i * 8 : (i + 1) * 8, j * LANES : (j + 1) * LANES] = v


def couple(off, at, known, solved, column, wide):
    def step(d, carry):
        at_rows = pl.ds(pl.multiple_of(d * BLOCK, BLOCK), BLOCK)
        drop = jnp.sum(off[at_rows, at : at + REACH] * known[pl.ds(d, 1), :], axis=1, keepdims=True)
        wide[at_rows, :] = jnp.broadcast_to(solved[at_rows, column : column + 1] - drop, (BLOCK, LANES))
        return carry

    lax.fori_loop(0, BLOCKS, step, 0, unroll=4)


def forward_low(pack, start, solved, residual, places, held, wide, named, sems):
    copies = [
        pltpu.make_async_copy(pack.at[:, AUX_AT + k * LANES : AUX_AT + (k + 1) * LANES], named.at[k], sems.at[k + 1])
        for k in range(2)
    ]
    copies.append(pltpu.make_async_copy(pack.at[:, 0:AUX_AT], held, sems.at[0]))
    for copy in copies:
        copy.start()
    residual[...] = start[...]
    for copy in copies:
        copy.wait()
    block = lax.broadcasted_iota(jnp.int32, (BLOCKS, REACH), 0)
    for level in range(5):
        quarters = [
            named.at[a][pl.ds(2 * level + k, BLOCKS, stride=BLOCK), :] for k in range(2) for a in range(2)
        ]
        chain = jnp.concatenate(quarters, axis=1).astype(jnp.int32) + (2 ** (level + 1) - 1) * LANES
        shift = jnp.where((chain < 3 * LANES) & (block < 16), 8 * LANES - LANES, 9 * LANES)
        places[level] = chain + shift
    for level in range(3):
        groups = 4 >> level
        first = FIRST[level]

        def write(at, value, level=level):
            wide[at : at + 64, :] = jnp.broadcast_to(value, (64, LANES))
            solved[at : at + 64, level : level + 1] = value

        matvec(
            held, DIAG_AT[level], groups, 1 << level,
            lambda c, first=first: residual[first + c : first + c + 1, :], write,
        )
        update = scatter_update(held, OFF_AT[level], wide, places.at[level], 8, 64)
        residual[8:72, :] = residual[8:72, :] - update


def forward_high(level, pack, summed, before, places, solved, residual, held, wide, sems):
    first = FIRST[level + 1]
    columns = COUNT[level] * LANES
    copy = pltpu.make_async_copy(
        pack.at[:, DIAG_AT[level] : DIAG_AT[level] + columns + REACH], held, sems.at[0]
    )
    copy.start()
    residual[...] = before[...]
    copy.wait()

    def write(at, value):
        wide[at : at + 64, :] = jnp.broadcast_to(value, (64, LANES))
        solved[at : at + 64, 0:1] = value

    matvec(held, 0, 1, COUNT[level], lambda c: summed[c : c + 1, :], write)
    update = scatter_update(held, columns, wide, places.at[level], first, SPACE - first)
    residual[first:SPACE, :] = residual[first:SPACE, :] - update


def top(pack, summed, partial, held, wide, sems):
    copy = pltpu.make_async_copy(pack.at[:, DIAG_AT[5] : DIAG_AT[5] + 32 * LANES], held, sems.at[0])
    copy.start()
    copy.wait()

    def write(at, value):
        wide[at : at + 64, :] = jnp.broadcast_to(value, (64, LANES))

    matvec(held, 0, 1, COUNT[5], lambda c: summed[c : c + 1, :], write)

    def write_row(c, value):
        partial[c : c + 1, :] = value

    matvec_transposed(held, 0, 1, COUNT[5], wide, write_row)


def backward_high(level, pack, places, solved, *rest):
    above = rest[: 5 - level]
    partial, held, wide, chain, known, sems = rest[5 - level :]
    columns = COUNT[level] * LANES
    copy = pltpu.make_async_copy(
        pack.at[:, DIAG_AT[level] : DIAG_AT[level] + columns + REACH], held, sems.at[0]
    )
    copy.start()
    for k, value in enumerate(above):
        chain[FIRST[5 - k] : FIRST[5 - k] + COUNT[5 - k], :] = value[...]
    gather_known(known, chain, places.at[level], FIRST[level + 1])
    copy.wait()
    couple(held, columns, known, solved, 0, wide)

    def write_row(c, value):
        partial[c : c + 1, :] = value

    matvec_transposed(held, 0, 1, COUNT[level], wide, write_row)


def backward_low(pack, places, solved, s5, s4, s3, out, held, wide, chain, known, sems):
    copy = pltpu.make_async_copy(pack.at[:, 0:AUX_AT], held, sems.at[0])
    copy.start()
    for level, value in ((5, s5), (4, s4), (3, s3)):
        chain[FIRST[level] : FIRST[level] + COUNT[level], :] = value[...]
    chain[0:16, :] = jnp.zeros((16, LANES), jnp.float32)
    for level in (2, 1, 0):
        gather_known(known, chain, places.at[level], FIRST[level + 1])
        if level == 2:
            copy.wait()
        couple(held, OFF_AT[level], known, solved, level, wide)

        def write_row(c, value, first=FIRST[level]):
            chain[first + c : first + c + 1, :] = value

        matvec_transposed(held, DIAG_AT[level], 4 >> level, 1 << level, wide, write_row)
    out[...] = chain[0:16, :]


def call(body, outs, scratch, hbm_first, args):
    vmem = pl.BlockSpec(memory_space=pltpu.VMEM)
    specs = [pl.BlockSpec(memory_space=pl.ANY) if k == 0 and hbm_first else vmem for k in range(len(args))]
    return pl.pallas_call(
        body,
        out_shape=outs,
        in_specs=specs,
        out_specs=jax.tree.map(lambda _: vmem, outs),
        scratch_shapes=scratch + [pltpu.SemaphoreType.DMA((3,))],
        compiler_params=pltpu.CompilerParams(vmem_limit_bytes=VMEM_LIMIT),
    )(*args)


def shape(*dims, kind=jnp.float32):
    return jax.ShapeDtypeStruct(dims, kind)


def sum_planes(value, bits):
    for bit in range(bits):
        size = lax.axis_size("z")
        value = value + lax.ppermute(value, "z", [(i, i ^ 1 << bit) for i in range(size)])
    return value


def local(rhs, diag_inverse, off_diagonal, rows_index):
    f32 = jnp.float32
    plane = lax.axis_index("z")
    pack = lax.all_gather(pack_local(diag_inverse, off_diagonal, rows_index), PLANE, axis=0, tiled=True)
    mine = lax.all_to_all(jnp.transpose(rhs, (1, 0, 2)), PLANE, 0, 0)
    mine = jnp.transpose(mine, (1, 0, 2)).reshape(6, 4, LANES)
    start = jnp.zeros((SPACE, LANES), f32)
    for level in range(6):
        place = FIRST[level] + (jnp.remainder(plane, 2 ** (level - 2)) * 4 if level > 2 else 0)
        start = lax.dynamic_update_slice(start, mine[level], (place, 0))

    wide = pltpu.VMEM((ROWS, LANES), f32)
    solved_low, residual, places = call(
        forward_low,
        (shape(ROWS, 8), shape(SPACE, LANES), shape(5, BLOCKS, REACH, kind=jnp.int32)),
        [pltpu.VMEM((ROWS, AUX_AT), f32), wide, pltpu.VMEM((2, ROWS, LANES), f32)],
        True,
        (pack, start),
    )
    solved = {}
    for level in (3, 4):
        first, count = FIRST[level], COUNT[level]
        summed = sum_planes(residual[first : first + count], level - 2)
        solved[level], residual = call(
            functools.partial(forward_high, level),
            (shape(ROWS, 8), shape(SPACE, LANES)),
            [pltpu.VMEM((ROWS, count * LANES + REACH), f32), wide],
            True,
            (pack, summed, residual, places),
        )
    summed = sum_planes(residual[FIRST[5] : SPACE], 3)
    partial = call(
        top, shape(32, LANES), [pltpu.VMEM((ROWS, 32 * LANES), f32), wide], True, (pack, summed)
    )
    above = [sum_planes(partial, 3)]
    chain, known = pltpu.VMEM((SPACE, LANES), f32), pltpu.VMEM((BLOCKS, REACH), f32)
    for level in (4, 3):
        count = COUNT[level]
        partial = call(
            functools.partial(backward_high, level),
            shape(count, LANES),
            [pltpu.VMEM((ROWS, count * LANES + REACH), f32), wide, chain, known],
            True,
            (pack, places, solved[level], *above),
        )
        above.append(sum_planes(partial, level - 2))
    low = call(
        backward_low,
        shape(16, LANES),
        [pltpu.VMEM((ROWS, AUX_AT), f32), wide, chain, known],
        True,
        (pack, places, solved_low, *above),
    )
    pieces = [low[0:4], low[8:12], low[12:16]]
    for level in (3, 4, 5):
        place = jnp.remainder(plane, 2 ** (level - 2)) * 4
        pieces.append(lax.dynamic_slice_in_dim(above[5 - level], place, 4, 0))
    out = jnp.stack(pieces).reshape(6, BLOCKS, BLOCK)
    out = lax.all_to_all(jnp.transpose(out, (1, 0, 2)), PLANE, 0, 0)
    return jnp.transpose(out, (1, 0, 2))


def solution(mesh):
    split = Mesh(mesh.devices.reshape(8, 4, 8), ("z", "x", "blk"))
    rows = ("z", "x", "blk")
    placed = (P(None, None, rows), P(rows, None), P(None, rows, None), P(None, rows, None))
    return jax.shard_map(
        local, mesh=split, in_specs=placed, out_specs=P(None, None, rows), check_vma=False
    )
```

```python
import functools

import jax
import jax.numpy as jnp
from jax import lax
from jax.experimental import pallas as pl
from jax.experimental.pallas import tpu as pltpu
from jax.sharding import Mesh
from jax.sharding import PartitionSpec as P

PLANE = ("x", "blk")
LANES = 128
BLOCK = 16
BLOCKS = 32
ROWS = BLOCK * BLOCKS
REACH = 512
SLOTS = 8
OWN = SLOTS * BLOCK
SPECIES = 4
FIRST = (0, 8, 12, 16, 24, 40)
COUNT = (4, 4, 4, 8, 16, 32)
SPACE = 72
PATH = 64
PARTS = 10
DIAG_AT = (512, 1152, 1920, 2944, 0, 2048)
OFF_AT = (640, 1408, 2432, 3968, 6144)
NAMED_AT = (0, 6656)
RHS_AT = 256
CUT = 1920
LOW = 4480
HIGH = 6912
LEVEL_AT = ((0, 1152), (1152, 1920), (1920, 2944), (2944, 4480))
MIB = 1024 * 1024


def pack_kernel(rhs, rows_index, diag_inverse, off_diagonal, high, low, first, second, sems):
    moves = [(diag_inverse.at[:, 1920:8064], high.at[:, 0:6144])]
    moves.append((off_diagonal.at[4], high.at[:, OFF_AT[4] : OFF_AT[4] + REACH]))
    for level in range(4):
        part, at = (first, 0) if level < 2 else (second, CUT)
        columns = 2**level * LANES
        diag = diag_inverse.at[:, columns - LANES : 2 * columns - LANES]
        for to, less in ((part, at), (low, 0)):
            first_at, second_at = DIAG_AT[level] - less, OFF_AT[level] - less
            moves.append((diag, to.at[:, first_at : first_at + columns]))
            moves.append((off_diagonal.at[level], to.at[:, second_at : second_at + REACH]))
    copies = [pltpu.make_async_copy(source, target, sems.at[k]) for k, (source, target) in enumerate(moves)]
    for copy in copies:
        copy.start()
    given = jnp.concatenate(
        [jnp.transpose(rhs[...].reshape(192, BLOCK)), jnp.zeros((BLOCK, 64), jnp.float32)], axis=1
    )
    for to in (first, low):
        to[:, RHS_AT : RHS_AT + 256] = given
    for to, at in ((first, NAMED_AT[0]), (low, NAMED_AT[0]), (high, NAMED_AT[1])):
        for level in range(5):
            for k in range(2):
                named = rows_index[level, :, k * 256 : (k + 1) * 256].astype(jnp.float32)
                to[2 * level + k : 2 * level + k + 1, at : at + 256] = named
        to[10:16, at : at + 256] = jnp.zeros((6, 256), jnp.float32)
    for copy in copies:
        copy.wait()


def matvec(diag, at, groups, chunks, read_row, write, rows=ROWS):
    size = rows // groups
    for k in range(groups):
        for start in range(k * size, (k + 1) * size, 64):
            total = None
            for c in range(chunks):
                term = diag[start : start + 64, at + c * LANES : at + (c + 1) * LANES] * read_row(k * chunks + c)
                total = term if total is None else total + term
            write(start, jnp.sum(total, axis=1, keepdims=True))


def matvec_transposed(diag, at, groups, chunks, wide, write, rows=ROWS):
    size = rows // groups
    for k in range(groups):
        for c in range(chunks):
            total = None
            for start in range(k * size, (k + 1) * size, 64):
                term = diag[start : start + 64, at + c * LANES : at + (c + 1) * LANES] * wide[start : start + 64, :]
                total = term if total is None else total + term
            write(k * chunks + c, jnp.sum(total, axis=0, keepdims=True))


def split(value):
    coarse = value.astype(jnp.bfloat16)
    return coarse, (value - coarse.astype(jnp.float32)).astype(jnp.bfloat16)


def one_hot(where, rows, first):
    names = lax.broadcasted_iota(jnp.int32, (rows, REACH), 0) + first
    return names == where


def block_rows(d):
    return pl.ds(pl.multiple_of(d * BLOCK, BLOCK), BLOCK)


def scatter_update(off, at, wide, place, first, height):
    def step(d, total):
        solved = wide[block_rows(d), :]
        solved = jnp.concatenate([solved] * (REACH // LANES), axis=1)
        update = jnp.sum(off[block_rows(d), at : at + REACH] * solved, axis=0, keepdims=True)
        where = place[pl.ds(d, 1), :]
        hit = one_hot(jnp.right_shift(where, 7), height, first)
        coarse = update.astype(jnp.bfloat16).astype(jnp.float32)
        left = jnp.concatenate(
            [jnp.where(hit, part, 0.0).astype(jnp.bfloat16) for part in (coarse, update - coarse)], axis=0
        )
        right = one_hot(jnp.bitwise_and(where, 127), LANES, 0).astype(jnp.bfloat16)
        return total + lax.dot_general(
            left, right, (((1,), (1,)), ((), ())), preferred_element_type=jnp.float32
        )

    total = lax.fori_loop(0, BLOCKS, step, jnp.zeros((2 * height, LANES), jnp.float32), unroll=4)
    return total[:height] + total[height:]


def couple(off, at, chain, place, first, solved, column, wide):
    height = SPACE - first
    table = jnp.concatenate(split(chain[first:SPACE, :]), axis=0)

    def step(d, carry):
        where = place[pl.ds(d, 1), :]
        right = one_hot(jnp.bitwise_and(where, 127), LANES, 0).astype(jnp.bfloat16)
        rows = jnp.dot(table, right, preferred_element_type=jnp.float32)
        hit = one_hot(jnp.right_shift(where, 7), height, first)
        known = jnp.sum(jnp.where(hit, rows[:height] + rows[height:], 0.0), axis=0, keepdims=True)
        drop = jnp.sum(off[block_rows(d), at : at + REACH] * known, axis=1, keepdims=True)
        wide[block_rows(d), :] = jnp.broadcast_to(
            solved[block_rows(d), column : column + 1] - drop, (BLOCK, LANES)
        )
        return carry

    lax.fori_loop(0, BLOCKS, step, 0, unroll=4)


def fetch(pack, held, sems, cuts):
    copies = []
    for k, (first, last, to) in enumerate(cuts):
        copies.append(
            pltpu.make_async_copy(pack.at[:, first:last], held.at[:, to : to + last - first], sems.at[k])
        )
        copies[-1].start()
    return copies


def fetch_named(pack, named, sems, at, which):
    first = NAMED_AT[which]
    copies = [
        pltpu.make_async_copy(pack.at[:, first + k * LANES : first + (k + 1) * LANES], named.at[k], sems.at[at + k])
        for k in range(2)
    ]
    for copy in copies:
        copy.start()
    return copies


def chain_position(named, level, blocks):
    quarters = [
        named.at[a][pl.ds(2 * level + k, blocks, stride=BLOCK), :] for k in range(2) for a in range(2)
    ]
    return jnp.concatenate(quarters, axis=1).astype(jnp.int32) + (2 ** (level + 1) - 1) * LANES


def find_places(named, level, places):
    chain = chain_position(named, level, BLOCKS)
    if level == 0:
        block = lax.broadcasted_iota(jnp.int32, (BLOCKS, REACH), 0)
        places[...] = chain + jnp.where((chain < 3 * LANES) & (block < 16), 7 * LANES, 9 * LANES)
    else:
        places[...] = chain + 9 * LANES


def fetch_parts(parts, level, held, sems):
    first, last = LEVEL_AT[level]
    less = 0 if level < 2 else CUT
    copies, at = [], 0
    for k, part in enumerate(parts):
        count = part.shape[0]
        copies.append(
            pltpu.make_async_copy(part.at[:, first - less : last - less], held.at[pl.ds(at, count), :], sems.at[k])
        )
        copies[-1].start()
        at += count
    return copies


def path_solve(level, read, held, place, wide, total):
    diag_at, off_at = DIAG_AT[level] - LEVEL_AT[level][0], OFF_AT[level] - LEVEL_AT[level][0]
    for n in range(SPECIES):

        def write(at, value, n=n):
            wide[n, at : at + 64, :] = jnp.broadcast_to(value, (64, LANES))

        matvec(held, diag_at, 1, 2**level, functools.partial(read, n), write, OWN)
    for d in range(SLOTS):
        where = place[d : d + 1, :]
        hit = one_hot(jnp.right_shift(where, 7), PATH, 0)
        right = one_hot(jnp.bitwise_and(where, 127), LANES, 0).astype(jnp.bfloat16)
        rows = slice(d * BLOCK, (d + 1) * BLOCK)
        left = []
        for n in range(SPECIES):
            solved = jnp.concatenate([wide[n, rows, :]] * (REACH // LANES), axis=1)
            update = jnp.sum(held[rows, off_at : off_at + REACH] * solved, axis=0, keepdims=True)
            coarse = update.astype(jnp.bfloat16).astype(jnp.float32)
            left += [jnp.where(hit, part, 0.0).astype(jnp.bfloat16) for part in (coarse, update - coarse)]
        product = lax.dot_general(
            jnp.concatenate(left, axis=0), right, (((1,), (1,)), ((), ())), preferred_element_type=jnp.float32
        )
        total[...] = product if d == 0 else total[...] + product


def path_update(level, before, total, path, ahead):
    count = 2 ** (level + 1)
    for n in range(SPECIES):
        at = 2 * n * PATH
        path[n * PATH : (n + 1) * PATH, :] = before[n * PATH : (n + 1) * PATH, :] - (
            total[at : at + PATH, :] + total[at + PATH : at + 2 * PATH, :]
        )
        if ahead is not None:
            ahead[n * count : (n + 1) * count, :] = path[n * PATH + count : n * PATH + 2 * count, :]


def path_first(*refs):
    parts = refs[:PARTS]
    here, path, ahead, r0, places, held, named, turned, wide, total, sems = refs[PARTS:]
    leaf, b = here[0], here[1]
    copies = fetch_parts(parts, 0, held, sems)
    path[...] = jnp.zeros((SPECIES * PATH, LANES), jnp.float32)
    lane = lax.broadcasted_iota(jnp.int32, (BLOCK, LANES), 1)
    row = lax.broadcasted_iota(jnp.int32, (BLOCK, LANES), 0)
    stands = []
    for core in (0, 1):
        for ahead_by in (0, 6, 2, 4):
            slot = jnp.bitwise_and(b + ahead_by, 7) ^ core
            stands.append(jnp.where(lane == row + slot * BLOCK, 1.0, 0.0).astype(jnp.bfloat16))
    order = jnp.concatenate(stands, axis=0)
    for copy in copies:
        copy.wait()
    flipped = jnp.transpose(held[:, RHS_AT : RHS_AT + 256])
    total_rows = None
    for _ in range(3):
        piece = flipped.astype(jnp.bfloat16)
        flipped = flipped - piece.astype(jnp.float32)
        rows = jnp.dot(piece, order, preferred_element_type=jnp.float32)
        total_rows = rows if total_rows is None else total_rows + rows
    turned[...] = total_rows
    for n in range(SPECIES):
        r0[n : n + 1, :] = turned[pl.ds(b * SPECIES + n, 1), :]
        for level in range(1, 6):
            at = n * PATH + 2**level + jnp.bitwise_and(leaf, 2**level - 1)
            path[pl.ds(at, 1), :] = turned[pl.ds(level * 32 + b * SPECIES + n, 1), :]
    named[0] = held[:, 0:LANES]
    named[1] = held[:, LANES : 2 * LANES]
    for level in range(4):
        places[level] = chain_position(named, level, SLOTS) + LANES
    path_solve(0, lambda n, c: r0[n : n + 1, :], held, places.at[0], wide, total)
    path_update(0, path, total, path, ahead)


def path_next(level, *refs):
    parts = refs[:PARTS]
    places, summed, before, path, ahead, held, wide, total, sems = refs[PARTS:]
    copies = fetch_parts(parts, level, held, sems)
    count = 2**level
    for copy in copies:
        copy.wait()
    path_solve(
        level, lambda n, c: summed[n * count + c : n * count + c + 1, :], held, places.at[level], wide, total
    )
    path_update(level, before, total, path, ahead)


def path_last(*refs):
    parts, (place, places, r0, r1, r2, summed, before, keep, send, t2, t3, path, *scratch) = refs[:PARTS], refs[PARTS:]
    path_next(3, *parts, places, summed, before, path, None, *scratch)
    x = place[0]
    even = 1.0 - (x & 1).astype(jnp.float32)
    for n in range(SPECIES):
        slot = n ^ x
        slot = slot ^ (slot >> 1)
        value = jnp.zeros((8, LANES), jnp.float32)
        row = lax.broadcasted_iota(jnp.int32, (8, LANES), 0)
        value = jnp.where(row == x, r0[n : n + 1, :], value)
        for k in range(2):
            value = jnp.where(row == 4 + 2 * (x >> 1) + k, r1[2 * n + k : 2 * n + k + 1, :] * even, value)

        @pl.when(slot < 2)
        def _(n=n, slot=slot, value=value):
            keep[slot, 0:48, :] = path[n * PATH + 16 : (n + 1) * PATH, :]
            keep[slot, 48:56, :] = value

        @pl.when(slot >= 2)
        def _(n=n, slot=slot, value=value):
            send[slot - 2, 0:48, :] = path[n * PATH + 16 : (n + 1) * PATH, :]
            send[slot - 2, 48:56, :] = value

    t2[...] = r2[pl.ds(x * 4, 4), :]
    t3[...] = summed[pl.ds(pl.multiple_of(x * 8, 8), 8), :]


def high_cuts(level):
    columns = COUNT[level] * LANES
    return [
        (DIAG_AT[level], DIAG_AT[level] + columns, 0),
        (OFF_AT[level], OFF_AT[level] + REACH, columns),
    ]


def forward_high(pack, summed, before, solved, residual, held, wide, named, places, sems):
    level, columns = 4, COUNT[4] * LANES
    named_copies = fetch_named(pack, named, sems, 6, 1)
    copies = fetch(pack, held, sems, high_cuts(level))

    def write(at, value):
        wide[at : at + 64, :] = jnp.broadcast_to(value, (64, LANES))
        solved[at : at + 64, 0:1] = value

    copies[0].wait()
    matvec(held, 0, 1, COUNT[level], lambda c: summed[c : c + 1, :], write)
    for copy in named_copies + copies[1:]:
        copy.wait()
    find_places(named, level, places)
    residual[...] = before[...] - scatter_update(held, columns, wide, places, FIRST[5], COUNT[5])


def top(pack, summed, partial, held, wide, sems):
    copies = []
    for k in range(4):
        rows = pl.ds(k * 128, 128)
        copies.append(
            pltpu.make_async_copy(
                pack.at[rows, DIAG_AT[5] : DIAG_AT[5] + 32 * LANES], held.at[rows, :], sems.at[k]
            )
        )
        copies[-1].start()
    for k in range(4):
        copies[k].wait()
        rows = slice(k * 128, (k + 1) * 128)

        def write(at, value, k=k):
            wide[k * 128 + at : k * 128 + at + 64, :] = jnp.broadcast_to(value, (64, LANES))

        matvec(held.at[rows, :], 0, 1, COUNT[5], lambda c: summed[c : c + 1, :], write, 128)

        def write_row(c, value, k=k):
            partial[c : c + 1, :] = value if k == 0 else partial[c : c + 1, :] + value

        matvec_transposed(held.at[rows, :], 0, 1, COUNT[5], wide.at[rows, :], write_row, 128)


def backward_high(level, pack, residual, *rest):
    above = rest[: 5 - level]
    partial, held, wide, chain, named, places, solved, sems = rest[5 - level :]
    columns = COUNT[level] * LANES
    named_copies = fetch_named(pack, named, sems, 6, level - 3)
    copies = fetch(pack, held, sems, high_cuts(level)[::-1])
    for k, value in enumerate(above):
        chain[FIRST[5 - k] : FIRST[5 - k] + COUNT[5 - k], :] = value[...]
    for copy in named_copies:
        copy.wait()
    find_places(named, level, places)
    if level == 4:
        solved = residual
    else:

        def write(at, value):
            solved[at : at + 64, 0:1] = value

        copies[1].wait()
        matvec(held, 0, 1, COUNT[level], lambda c: residual[c : c + 1, :], write)
    copies[0].wait()
    couple(held, columns, chain, places, FIRST[level + 1], solved, 0, wide)
    if level == 4:
        copies[1].wait()

    def write_row(c, value):
        partial[c : c + 1, :] = value

    matvec_transposed(held, 0, 1, COUNT[level], wide, write_row)


def backward_low(pack, r01, r2, s5, s4, s3, out, held, wide, chain, named, places, solved, sems):
    named_copies = fetch_named(pack, named, sems, 6, 0)
    cuts = []
    for level in (2, 1, 0):
        diag_at, off_at = DIAG_AT[level], OFF_AT[level]
        cuts.append((diag_at, diag_at + LANES * 2**level, LANES * (2**level - 1)))
        cuts.append((off_at, off_at + REACH, 896 + REACH * level))
    copies = fetch(pack, held, sems, cuts)
    for level, value in ((5, s5), (4, s4), (3, s3)):
        chain[FIRST[level] : FIRST[level] + COUNT[level], :] = value[...]
    chain[0:16, :] = jnp.zeros((16, LANES), jnp.float32)
    for copy in named_copies:
        copy.wait()
    for k, level in enumerate((2, 1, 0)):
        find_places(named, level, places)

        def write(at, value):
            solved[at : at + 64, 0:1] = value

        def read(c, level=level):
            return r2[c : c + 1, :] if level == 2 else r01[4 * level + c : 4 * level + c + 1, :]

        copies[2 * k].wait()
        matvec(held, LANES * (2**level - 1), 4 >> level, 1 << level, read, write)
        copies[2 * k + 1].wait()
        couple(held, 896 + REACH * level, chain, places, 8, solved, 0, wide)

        def write_row(c, value, first=FIRST[level]):
            chain[first + c : first + c + 1, :] = value

        matvec_transposed(held, LANES * (2**level - 1), 4 >> level, 1 << level, wide, write_row)
    out[...] = chain[0:16, :]


def call(body, outs, scratch, args, far=1, scalar=(), sems=8):
    vmem = pl.BlockSpec(memory_space=pltpu.VMEM)
    smem = pl.BlockSpec(memory_space=pltpu.SMEM)
    hbm = pl.BlockSpec(memory_space=pltpu.HBM)
    specs = [hbm if k < far else smem if k in scalar else vmem for k in range(len(args))]
    return pl.pallas_call(
        body,
        out_shape=outs,
        in_specs=specs,
        out_specs=jax.tree.map(lambda _: vmem, outs),
        scratch_shapes=scratch + [pltpu.SemaphoreType.DMA((sems,))],
        compiler_params=pltpu.CompilerParams(vmem_limit_bytes=(52 if far == 1 else 6) * MIB),
    )(*args)


def shape(*dims, kind=jnp.float32):
    return jax.ShapeDtypeStruct(dims, kind)


def moved(value, axis, to):
    size = lax.axis_size(axis)
    return lax.ppermute(value, axis, [(i, to(i)) for i in range(size)])


def near_x(i):
    return 3 - i


def far_z(i):
    return (i + 5) % 8 if i % 2 else (i + 3) % 8


def sum_leaf(value, first, last):
    steps = [("x", lambda i: i ^ 1), ("x", near_x), ("z", lambda i: i ^ 1)]
    if last < 5:
        steps.append(("z", lambda i: i ^ 2))
    else:
        steps.append(("z", lambda i: (i + 1) % 8 if i % 2 else (i + 7) % 8))
        steps.append(("z", far_z))
    for axis, to in steps[first:last]:
        value = value + moved(value, axis, to)
    return value


def local(rhs, diag_inverse, off_diagonal, rows_index):
    f32 = jnp.float32
    x, z = lax.axis_index("x"), lax.axis_index("z")
    leaf = z * 4 + x
    hbm, vmem = pl.BlockSpec(memory_space=pltpu.HBM), pl.BlockSpec(memory_space=pltpu.VMEM)
    high, low, first, second = pl.pallas_call(
        pack_kernel,
        out_shape=(shape(BLOCK, HIGH), shape(BLOCK, LOW), shape(BLOCK, CUT), shape(BLOCK, LOW - CUT)),
        in_specs=[vmem, vmem, hbm, hbm],
        out_specs=(vmem,) * 4,
        scratch_shapes=[pltpu.SemaphoreType.DMA((18,))],
        compiler_params=pltpu.CompilerParams(vmem_limit_bytes=6 * MIB),
    )(rhs, rows_index, diag_inverse, off_diagonal)
    high = lax.all_gather(high, PLANE, axis=0, tiled=True)
    low = lax.all_gather(low, PLANE, axis=0, tiled=True)

    def group_rows(own):
        down = moved(own, "blk", lambda i: (i + 2) % SLOTS)
        up = moved(own, "blk", lambda i: (i + 6) % SLOTS)
        half = BLOCK // 2
        across = [
            moved(down[:half], "blk", lambda i: (i + 2) % SLOTS),
            moved(up[half:], "blk", lambda i: (i + 6) % SLOTS),
        ]
        here = (own, down, up, *across)
        return here + tuple(moved(part, "blk", lambda i: i ^ 1) for part in here)

    first = group_rows(first)
    second = group_rows(lax.optimization_barrier((second, first[-1]))[0])

    def path_scratch(level, *more):
        return [
            pltpu.VMEM((OWN, LEVEL_AT[level][1] - LEVEL_AT[level][0]), f32),
            *more,
            pltpu.VMEM((SPECIES, OWN, LANES), f32),
            pltpu.VMEM((SPECIES * 2 * PATH, LANES), f32),
        ]

    here = jnp.stack([leaf, lax.axis_index("blk")]).astype(jnp.int32)
    path, ahead, r0, places = call(
        path_first,
        (
            shape(SPECIES * PATH, LANES), shape(SPECIES * 2, LANES), shape(SPECIES, LANES),
            shape(4, SLOTS, REACH, kind=jnp.int32),
        ),
        path_scratch(0, pltpu.VMEM((2, OWN, LANES), f32), pltpu.VMEM((256, LANES), f32)),
        (*first, here),
        far=PARTS,
        scalar=(PARTS,),
        sems=PARTS,
    )
    waiting = [r0, sum_leaf(ahead, 0, 1)]
    for level in (1, 2):
        path, ahead = call(
            functools.partial(path_next, level),
            (shape(SPECIES * PATH, LANES), shape(SPECIES * 2 ** (level + 1), LANES)),
            path_scratch(level),
            (*(first if level < 2 else second), places, waiting[level], path),
            far=PARTS,
            sems=PARTS,
        )
        waiting.append(sum_leaf(ahead, 0, level + 1))
    keep, send, r2, r3 = call(
        path_last,
        (shape(2, 56, LANES), shape(2, 56, LANES), shape(4, LANES), shape(8, LANES)),
        [pltpu.VMEM((SPECIES * PATH, LANES), f32)] + path_scratch(3),
        (*second, x.astype(jnp.int32).reshape(1), places, *waiting, path),
        far=PARTS,
        scalar=(PARTS,),
        sems=PARTS,
    )
    keep = keep + moved(send, "x", near_x)
    turned = keep[0] + moved(keep[1], "x", lambda i: i ^ 1)
    r4 = sum_leaf(turned[0:16], 2, 4)

    wide, chain = pltpu.VMEM((ROWS, LANES), f32), pltpu.VMEM((SPACE, LANES), f32)
    named, places = pltpu.VMEM((2, ROWS, LANES), f32), pltpu.VMEM((BLOCKS, REACH), jnp.int32)
    solved = pltpu.VMEM((ROWS, 8), f32)
    y4, r5 = call(
        forward_high,
        (shape(ROWS, 8), shape(32, LANES)),
        [pltpu.VMEM((ROWS, 16 * LANES + REACH), f32), wide, named, places],
        (high, r4, turned[16:48]),
    )
    r5 = sum_leaf(r5, 2, 5)
    partial = call(top, shape(32, LANES), [pltpu.VMEM((ROWS, 32 * LANES), f32), wide], (high, r5))
    known = [sum_leaf(partial, 2, 5)]
    for level, from_rows in ((4, y4), (3, r3)):
        count = COUNT[level]
        partial = call(
            functools.partial(backward_high, level),
            shape(count, LANES),
            [pltpu.VMEM((ROWS, count * LANES + REACH), f32), wide, chain, named, places, solved],
            (high if level == 4 else low, from_rows, *known),
        )
        known.append(sum_leaf(partial, 2, level))
    last = call(
        backward_low,
        shape(16, LANES),
        [pltpu.VMEM((ROWS, 896 + 3 * REACH), f32), wide, chain, named, places, solved],
        (low, turned[48:56], r2, *known),
    )
    pieces = [last[0:4], last[8:12], last[12:16]]
    for level in (3, 4, 5):
        place = jnp.remainder(z, 2 ** (level - 2)) * 4
        pieces.append(lax.dynamic_slice_in_dim(known[5 - level], place, 4, 0))
    out = jnp.stack(pieces).reshape(6, BLOCKS, BLOCK)
    out = lax.all_to_all(jnp.transpose(out, (1, 0, 2)), PLANE, 0, 0)
    return jnp.transpose(out.reshape(SPECIES, SLOTS, 6, BLOCK), (2, 1, 0, 3)).reshape(6, BLOCKS, BLOCK)


def solution(mesh):
    cut = Mesh(mesh.devices.reshape(8, 4, 8), ("z", "x", "blk"))
    rows = ("z", "x", "blk")
    placed = (P(None, None, rows), P(rows, None), P(None, rows, None), P(None, rows, None))
    return jax.shard_map(
        local, mesh=cut, in_specs=placed, out_specs=P(None, None, rows), check_vma=False
    )
```

```python
import functools

import jax
import jax.numpy as jnp
from jax import lax
from jax.experimental import pallas as pl
from jax.experimental.pallas import tpu as pltpu
from jax.sharding import Mesh
from jax.sharding import PartitionSpec as P

PLANE = ("x", "blk")
LANES = 128
BLOCK = 16
BLOCKS = 32
ROWS = BLOCK * BLOCKS
REACH = 512
SLOTS = 8
OWN = SLOTS * BLOCK
SPECIES = 4
FIRST = (0, 8, 12, 16, 24, 40)
COUNT = (4, 4, 4, 8, 16, 32)
SPACE = 72
PATH = 64
PARTS = 10
RHS_AT = 0
NAMED_AT = 256
DIAG_AT = (512, 1152, 1920, 2944)
OFF_AT = (640, 1408, 2432, 3968)
CUT = 1920
GROUP = 4480
LOW = 2688
HIGH = 8448
PLANE_DIAG_AT = (256, 896, 1664, 0, 1024, 3072)
PLANE_OFF_AT = (384, 1152, 2176, 7168, 7680)
PLANE_NAMED_AT = (0, 8192)
LEVEL_AT = ((0, 1152), (1152, 1920), (1920, 2944), (2944, 4480))
MIB = 1024 * 1024


def store_named(rows_index, to, at):
    for level in range(5):
        for k in range(2):
            named = rows_index[level, :, k * 256 : (k + 1) * 256].astype(jnp.float32)
            to[2 * level + k : 2 * level + k + 1, at : at + 256] = named
    to[10:16, at : at + 256] = jnp.zeros((6, 256), jnp.float32)


def start_all(moves, sems):
    copies = [pltpu.make_async_copy(source, target, sems.at[k]) for k, (source, target) in enumerate(moves)]
    for copy in copies:
        copy.start()
    return copies


def pack_high(rows_index, diag_inverse, off_diagonal, high, sems):
    moves = [(diag_inverse.at[:, 896:8064], high.at[:, 0:7168])]
    for level in (3, 4):
        at = PLANE_OFF_AT[level]
        moves.append((off_diagonal.at[level], high.at[:, at : at + REACH]))
    copies = start_all(moves, sems)
    store_named(rows_index, high, PLANE_NAMED_AT[1])
    for copy in copies:
        copy.wait()


def pack_low(rhs, rows_index, diag_inverse, off_diagonal, low, first, second, sems):
    moves = []
    for level in range(4):
        part, less = (first, 0) if level < 2 else (second, CUT)
        columns = 2**level * LANES
        diag = diag_inverse.at[:, columns - LANES : 2 * columns - LANES]
        targets = [(part, DIAG_AT[level] - less, OFF_AT[level] - less)]
        if level < 3:
            targets.append((low, PLANE_DIAG_AT[level], PLANE_OFF_AT[level]))
        for to, diag_at, off_at in targets:
            moves.append((diag, to.at[:, diag_at : diag_at + columns]))
            moves.append((off_diagonal.at[level], to.at[:, off_at : off_at + REACH]))
    copies = start_all(moves, sems)
    first[:, RHS_AT : RHS_AT + 256] = jnp.concatenate(
        [jnp.transpose(rhs[...].reshape(192, BLOCK)), jnp.zeros((BLOCK, 64), jnp.float32)], axis=1
    )
    store_named(rows_index, first, NAMED_AT)
    store_named(rows_index, low, PLANE_NAMED_AT[0])
    for copy in copies:
        copy.wait()


def matvec(diag, at, groups, chunks, read_row, write, rows=ROWS):
    size = rows // groups
    for k in range(groups):
        for start in range(k * size, (k + 1) * size, 64):
            total = None
            for c in range(chunks):
                term = diag[start : start + 64, at + c * LANES : at + (c + 1) * LANES] * read_row(k * chunks + c)
                total = term if total is None else total + term
            write(start, jnp.sum(total, axis=1, keepdims=True))


def matvec_transposed(diag, at, groups, chunks, wide, write, rows=ROWS):
    size = rows // groups
    for k in range(groups):
        for c in range(chunks):
            total = None
            for start in range(k * size, (k + 1) * size, 64):
                term = diag[start : start + 64, at + c * LANES : at + (c + 1) * LANES] * wide[start : start + 64, :]
                total = term if total is None else total + term
            write(k * chunks + c, jnp.sum(total, axis=0, keepdims=True))


def split(value):
    coarse = value.astype(jnp.bfloat16)
    return coarse, (value - coarse.astype(jnp.float32)).astype(jnp.bfloat16)


def rows_iota(rows, first):
    return lax.broadcasted_iota(jnp.int32, (rows, REACH), 0) + first


def small(whole):
    return whole.astype(jnp.float32).astype(jnp.bfloat16)


def pick(hit, value):
    return jnp.where(hit, value, jnp.zeros((), jnp.bfloat16))


def lane_one_hot(where, lanes):
    return pick(lanes == small(jnp.bitwise_and(where, 127)), jnp.ones((), jnp.bfloat16))


def block_rows(d):
    return pl.ds(pl.multiple_of(d * BLOCK, BLOCK), BLOCK)


def scatter_update(off, at, wide, place, first, height):
    names, lanes = small(rows_iota(height, first)), small(rows_iota(LANES, 0))

    def step(d, total):
        solved = wide[block_rows(d), :]
        solved = jnp.concatenate([solved] * (REACH // LANES), axis=1)
        update = jnp.sum(off[block_rows(d), at : at + REACH] * solved, axis=0, keepdims=True)
        where = place[pl.ds(d, 1), :]
        hit = names == small(jnp.right_shift(where, 7))
        left = jnp.concatenate([pick(hit, part) for part in split(update)], axis=0)
        return total + lax.dot_general(
            left, lane_one_hot(where, lanes), (((1,), (1,)), ((), ())), preferred_element_type=jnp.float32
        )

    total = lax.fori_loop(0, BLOCKS, step, jnp.zeros((2 * height, LANES), jnp.float32), unroll=BLOCKS)
    return total[:height] + total[height:]


def couple(off, at, chain, place, first, solved, column, wide):
    height = SPACE - first
    table = jnp.concatenate(split(chain[first:SPACE, :]), axis=0)
    names, lanes = rows_iota(height, first), small(rows_iota(LANES, 0))

    def step(d, carry):
        where = place[pl.ds(d, 1), :]
        rows = jnp.dot(table, lane_one_hot(where, lanes), preferred_element_type=jnp.float32)
        hit = names == jnp.right_shift(where, 7)
        known = jnp.sum(jnp.where(hit, rows[:height] + rows[height:], 0.0), axis=0, keepdims=True)
        drop = jnp.sum(off[block_rows(d), at : at + REACH] * known, axis=1, keepdims=True)
        wide[block_rows(d), :] = jnp.broadcast_to(
            solved[block_rows(d), column : column + 1] - drop, (BLOCK, LANES)
        )
        return carry

    lax.fori_loop(0, BLOCKS, step, 0, unroll=BLOCKS)


def fetch(pack, held, sems, cuts):
    copies = []
    for k, (first, last, to) in enumerate(cuts):
        copies.append(
            pltpu.make_async_copy(pack.at[:, first:last], held.at[:, to : to + last - first], sems.at[k])
        )
        copies[-1].start()
    return copies


def fetch_named(pack, named, sems, at, which):
    first = PLANE_NAMED_AT[which]
    copies = [
        pltpu.make_async_copy(pack.at[:, first + k * LANES : first + (k + 1) * LANES], named.at[k], sems.at[at + k])
        for k in range(2)
    ]
    for copy in copies:
        copy.start()
    return copies


def chain_position(named, level, blocks):
    quarters = [
        named.at[a][pl.ds(2 * level + k, blocks, stride=BLOCK), :] for k in range(2) for a in range(2)
    ]
    return jnp.concatenate(quarters, axis=1).astype(jnp.int32) + (2 ** (level + 1) - 1) * LANES


def find_places(named, level, places):
    chain = chain_position(named, level, BLOCKS)
    if level == 0:
        block = lax.broadcasted_iota(jnp.int32, (BLOCKS, REACH), 0)
        places[...] = chain + jnp.where((chain < 3 * LANES) & (block < 16), 7 * LANES, 9 * LANES)
    else:
        places[...] = chain + 9 * LANES


def fetch_parts(parts, level, held, sems):
    first, last = LEVEL_AT[level]
    less = 0 if level < 2 else CUT
    copies, at = [], 0
    for k, part in enumerate(parts):
        count = part.shape[0]
        copies.append(
            pltpu.make_async_copy(part.at[:, first - less : last - less], held.at[pl.ds(at, count), :], sems.at[k])
        )
        copies[-1].start()
        at += count
    return copies


def path_solve(level, read, held, place, wide, total):
    diag_at, off_at = DIAG_AT[level] - LEVEL_AT[level][0], OFF_AT[level] - LEVEL_AT[level][0]
    for n in range(SPECIES):

        def write(at, value, n=n):
            wide[n, at : at + 64, :] = jnp.broadcast_to(value, (64, LANES))

        matvec(held, diag_at, 1, 2**level, functools.partial(read, n), write, OWN)
    names, lanes = small(rows_iota(PATH, 0)), small(rows_iota(LANES, 0))
    for d in range(SLOTS):
        where = place[d : d + 1, :]
        hit = names == small(jnp.right_shift(where, 7))
        right = lane_one_hot(where, lanes)
        rows = slice(d * BLOCK, (d + 1) * BLOCK)
        left = []
        for n in range(SPECIES):
            solved = jnp.concatenate([wide[n, rows, :]] * (REACH // LANES), axis=1)
            update = jnp.sum(held[rows, off_at : off_at + REACH] * solved, axis=0, keepdims=True)
            left += [pick(hit, part) for part in split(update)]
        product = lax.dot_general(
            jnp.concatenate(left, axis=0), right, (((1,), (1,)), ((), ())), preferred_element_type=jnp.float32
        )
        total[...] = product if d == 0 else total[...] + product


def path_update(level, before, total, path, ahead):
    count = 2 ** (level + 1)
    for n in range(SPECIES):
        at = 2 * n * PATH
        path[n * PATH : (n + 1) * PATH, :] = before[n * PATH : (n + 1) * PATH, :] - (
            total[at : at + PATH, :] + total[at + PATH : at + 2 * PATH, :]
        )
        if ahead is not None:
            ahead[n * count : (n + 1) * count, :] = path[n * PATH + count : n * PATH + 2 * count, :]


def path_first(*refs):
    parts = refs[:PARTS]
    here, path, ahead, r0, places, held, named, turned, wide, total, sems = refs[PARTS:]
    leaf, b = here[0], here[1]
    copies = fetch_parts(parts, 0, held, sems)
    path[...] = jnp.zeros((SPECIES * PATH, LANES), jnp.float32)
    lane = lax.broadcasted_iota(jnp.int32, (BLOCK, LANES), 1)
    row = lax.broadcasted_iota(jnp.int32, (BLOCK, LANES), 0)
    stands = []
    for core in (0, 1):
        for ahead_by in (0, 6, 2, 4):
            slot = jnp.bitwise_and(b + ahead_by, 7) ^ core
            stands.append(jnp.where(lane == row + slot * BLOCK, 1.0, 0.0).astype(jnp.bfloat16))
    order = jnp.concatenate(stands, axis=0)
    for copy in copies:
        copy.wait()
    flipped = jnp.transpose(held[:, RHS_AT : RHS_AT + 256])
    total_rows = None
    for _ in range(3):
        piece = flipped.astype(jnp.bfloat16)
        flipped = flipped - piece.astype(jnp.float32)
        rows = jnp.dot(piece, order, preferred_element_type=jnp.float32)
        total_rows = rows if total_rows is None else total_rows + rows
    turned[...] = total_rows
    for n in range(SPECIES):
        r0[n : n + 1, :] = turned[pl.ds(b * SPECIES + n, 1), :]
        for level in range(1, 6):
            at = n * PATH + 2**level + jnp.bitwise_and(leaf, 2**level - 1)
            path[pl.ds(at, 1), :] = turned[pl.ds(level * 32 + b * SPECIES + n, 1), :]
    for k in range(2):
        named[k] = held[:, NAMED_AT + k * LANES : NAMED_AT + (k + 1) * LANES]
    for level in range(4):
        places[level] = chain_position(named, level, SLOTS) + LANES
    path_solve(0, lambda n, c: r0[n : n + 1, :], held, places.at[0], wide, total)
    path_update(0, path, total, path, ahead)


def path_next(level, *refs):
    parts = refs[:PARTS]
    places, summed, before, path, ahead, held, wide, total, sems = refs[PARTS:]
    copies = fetch_parts(parts, level, held, sems)
    count = 2**level
    for copy in copies:
        copy.wait()
    path_solve(
        level, lambda n, c: summed[n * count + c : n * count + c + 1, :], held, places.at[level], wide, total
    )
    path_update(level, before, total, path, ahead)


def path_last(*refs):
    parts, (place, places, r0, r1, r2, summed, before, keep, send, t2, t3, path, *scratch) = refs[:PARTS], refs[PARTS:]
    path_next(3, *parts, places, summed, before, path, None, *scratch)
    x = place[0]
    even = 1.0 - (x & 1).astype(jnp.float32)
    for n in range(SPECIES):
        slot = n ^ x
        slot = slot ^ (slot >> 1)
        value = jnp.zeros((8, LANES), jnp.float32)
        row = lax.broadcasted_iota(jnp.int32, (8, LANES), 0)
        value = jnp.where(row == x, r0[n : n + 1, :], value)
        for k in range(2):
            value = jnp.where(row == 4 + 2 * (x >> 1) + k, r1[2 * n + k : 2 * n + k + 1, :] * even, value)

        @pl.when(slot < 2)
        def _(n=n, slot=slot, value=value):
            keep[slot, 0:48, :] = path[n * PATH + 16 : (n + 1) * PATH, :]
            keep[slot, 48:56, :] = value

        @pl.when(slot >= 2)
        def _(n=n, slot=slot, value=value):
            send[slot - 2, 0:48, :] = path[n * PATH + 16 : (n + 1) * PATH, :]
            send[slot - 2, 48:56, :] = value

    t2[...] = r2[pl.ds(x * 4, 4), :]
    t3[...] = summed[pl.ds(pl.multiple_of(x * 8, 8), 8), :]


def high_cuts(level):
    columns = COUNT[level] * LANES
    return [
        (PLANE_DIAG_AT[level], PLANE_DIAG_AT[level] + columns, 0),
        (PLANE_OFF_AT[level], PLANE_OFF_AT[level] + REACH, columns),
    ]


def forward_high(pack, summed, before, solved, residual, held, wide, named, places, sems):
    level, columns = 4, COUNT[4] * LANES
    named_copies = fetch_named(pack, named, sems, 6, 1)
    copies = fetch(pack, held, sems, high_cuts(level))

    def write(at, value):
        wide[at : at + 64, :] = jnp.broadcast_to(value, (64, LANES))
        solved[at : at + 64, 0:1] = value

    copies[0].wait()
    matvec(held, 0, 1, COUNT[level], lambda c: summed[c : c + 1, :], write)
    for copy in named_copies + copies[1:]:
        copy.wait()
    find_places(named, level, places)
    residual[...] = before[...] - scatter_update(held, columns, wide, places, FIRST[5], COUNT[5])


def top(pack, summed, partial, held, wide, sems):
    copies = []
    for k in range(4):
        rows = pl.ds(k * 128, 128)
        copies.append(
            pltpu.make_async_copy(
                pack.at[rows, PLANE_DIAG_AT[5] : PLANE_DIAG_AT[5] + 32 * LANES], held.at[rows, :], sems.at[k]
            )
        )
        copies[-1].start()
    for k in range(4):
        copies[k].wait()
        rows = slice(k * 128, (k + 1) * 128)

        def write(at, value, k=k):
            wide[k * 128 + at : k * 128 + at + 64, :] = jnp.broadcast_to(value, (64, LANES))

        matvec(held.at[rows, :], 0, 1, COUNT[5], lambda c: summed[c : c + 1, :], write, 128)

        def write_row(c, value, k=k):
            partial[c : c + 1, :] = value if k == 0 else partial[c : c + 1, :] + value

        matvec_transposed(held.at[rows, :], 0, 1, COUNT[5], wide.at[rows, :], write_row, 128)


def backward_high(level, pack, residual, *rest):
    above = rest[: 5 - level]
    partial, held, wide, chain, named, places, solved, sems = rest[5 - level :]
    columns = COUNT[level] * LANES
    named_copies = fetch_named(pack, named, sems, 6, 1)
    copies = fetch(pack, held, sems, high_cuts(level)[::-1])
    for k, value in enumerate(above):
        chain[FIRST[5 - k] : FIRST[5 - k] + COUNT[5 - k], :] = value[...]
    for copy in named_copies:
        copy.wait()
    find_places(named, level, places)
    if level == 4:
        solved = residual
    else:

        def write(at, value):
            solved[at : at + 64, 0:1] = value

        copies[1].wait()
        matvec(held, 0, 1, COUNT[level], lambda c: residual[c : c + 1, :], write)
    copies[0].wait()
    couple(held, columns, chain, places, FIRST[level + 1], solved, 0, wide)
    if level == 4:
        copies[1].wait()

    def write_row(c, value):
        partial[c : c + 1, :] = value

    matvec_transposed(held, 0, 1, COUNT[level], wide, write_row)


def backward_low(pack, r01, r2, s5, s4, s3, out, held, wide, chain, named, places, solved, sems):
    named_copies = fetch_named(pack, named, sems, 6, 0)
    cuts = []
    for level in (2, 1, 0):
        diag_at, off_at = PLANE_DIAG_AT[level], PLANE_OFF_AT[level]
        cuts.append((diag_at, diag_at + LANES * 2**level, LANES * (2**level - 1)))
        cuts.append((off_at, off_at + REACH, 896 + REACH * level))
    copies = fetch(pack, held, sems, cuts)
    for level, value in ((5, s5), (4, s4), (3, s3)):
        chain[FIRST[level] : FIRST[level] + COUNT[level], :] = value[...]
    chain[0:16, :] = jnp.zeros((16, LANES), jnp.float32)
    for copy in named_copies:
        copy.wait()
    for k, level in enumerate((2, 1, 0)):
        find_places(named, level, places)

        def write(at, value):
            solved[at : at + 64, 0:1] = value

        def read(c, level=level):
            return r2[c : c + 1, :] if level == 2 else r01[4 * level + c : 4 * level + c + 1, :]

        copies[2 * k].wait()
        matvec(held, LANES * (2**level - 1), 4 >> level, 1 << level, read, write)
        copies[2 * k + 1].wait()
        couple(held, 896 + REACH * level, chain, places, 8, solved, 0, wide)

        def write_row(c, value, first=FIRST[level]):
            chain[first + c : first + c + 1, :] = value

        matvec_transposed(held, LANES * (2**level - 1), 4 >> level, 1 << level, wide, write_row)
    out[...] = chain[0:16, :]


def call(body, outs, scratch, args, far=1, scalar=(), sems=8):
    vmem = pl.BlockSpec(memory_space=pltpu.VMEM)
    smem = pl.BlockSpec(memory_space=pltpu.SMEM)
    hbm = pl.BlockSpec(memory_space=pltpu.HBM)
    specs = [hbm if k < far else smem if k in scalar else vmem for k in range(len(args))]
    return pl.pallas_call(
        body,
        out_shape=outs,
        in_specs=specs,
        out_specs=jax.tree.map(lambda _: vmem, outs),
        scratch_shapes=scratch + [pltpu.SemaphoreType.DMA((sems,))],
        compiler_params=pltpu.CompilerParams(vmem_limit_bytes=(52 if far == 1 else 6) * MIB),
    )(*args)


def shape(*dims, kind=jnp.float32):
    return jax.ShapeDtypeStruct(dims, kind)


def moved(value, axis, to):
    size = lax.axis_size(axis)
    return lax.ppermute(value, axis, [(i, to(i)) for i in range(size)])


def near_x(i):
    return 3 - i


def far_z(i):
    return (i + 5) % 8 if i % 2 else (i + 3) % 8


def sum_leaf(value, first, last):
    steps = [("x", lambda i: i ^ 1), ("x", near_x), ("z", lambda i: i ^ 1)]
    if last < 5:
        steps.append(("z", lambda i: i ^ 2))
    else:
        steps.append(("z", lambda i: (i + 1) % 8 if i % 2 else (i + 7) % 8))
        steps.append(("z", far_z))
    for axis, to in steps[first:last]:
        value = value + moved(value, axis, to)
    return value


def local(rhs, diag_inverse, off_diagonal, rows_index):
    f32 = jnp.float32
    x, z = lax.axis_index("x"), lax.axis_index("z")
    leaf = z * 4 + x
    hbm, vmem = pl.BlockSpec(memory_space=pltpu.HBM), pl.BlockSpec(memory_space=pltpu.VMEM)
    high = pl.pallas_call(
        pack_high,
        out_shape=shape(BLOCK, HIGH),
        in_specs=[vmem, hbm, hbm],
        out_specs=vmem,
        scratch_shapes=[pltpu.SemaphoreType.DMA((3,))],
        compiler_params=pltpu.CompilerParams(vmem_limit_bytes=6 * MIB),
    )(rows_index, diag_inverse, off_diagonal)
    low, first, second = pl.pallas_call(
        pack_low,
        out_shape=(shape(BLOCK, LOW), shape(BLOCK, CUT), shape(BLOCK, GROUP - CUT)),
        in_specs=[vmem, vmem, hbm, hbm],
        out_specs=(vmem,) * 3,
        scratch_shapes=[pltpu.SemaphoreType.DMA((14,))],
        compiler_params=pltpu.CompilerParams(vmem_limit_bytes=6 * MIB),
    )(rhs, rows_index, diag_inverse, off_diagonal)
    high = lax.all_gather(high, PLANE, axis=0, tiled=True)
    low = lax.all_gather(low, PLANE, axis=0, tiled=True)

    def group_rows(own):
        down = moved(own, "blk", lambda i: (i + 2) % SLOTS)
        up = moved(own, "blk", lambda i: (i + 6) % SLOTS)
        half = BLOCK // 2
        across = [
            moved(down[:half], "blk", lambda i: (i + 2) % SLOTS),
            moved(up[half:], "blk", lambda i: (i + 6) % SLOTS),
        ]
        here = (own, down, up, *across)
        return here + tuple(moved(part, "blk", lambda i: i ^ 1) for part in here)

    first = group_rows(first)
    second = group_rows(lax.optimization_barrier((second, first[-1]))[0])

    def path_scratch(level, *more):
        return [
            pltpu.VMEM((OWN, LEVEL_AT[level][1] - LEVEL_AT[level][0]), f32),
            *more,
            pltpu.VMEM((SPECIES, OWN, LANES), f32),
            pltpu.VMEM((SPECIES * 2 * PATH, LANES), f32),
        ]

    here = jnp.stack([leaf, lax.axis_index("blk")]).astype(jnp.int32)
    path, ahead, r0, places = call(
        path_first,
        (
            shape(SPECIES * PATH, LANES), shape(SPECIES * 2, LANES), shape(SPECIES, LANES),
            shape(4, SLOTS, REACH, kind=jnp.int32),
        ),
        path_scratch(0, pltpu.VMEM((2, OWN, LANES), f32), pltpu.VMEM((256, LANES), f32)),
        (*first, here),
        far=PARTS,
        scalar=(PARTS,),
        sems=PARTS,
    )
    waiting = [r0, sum_leaf(ahead, 0, 1)]
    for level in (1, 2):
        path, ahead = call(
            functools.partial(path_next, level),
            (shape(SPECIES * PATH, LANES), shape(SPECIES * 2 ** (level + 1), LANES)),
            path_scratch(level),
            (*(first if level < 2 else second), places, waiting[level], path),
            far=PARTS,
            sems=PARTS,
        )
        waiting.append(sum_leaf(ahead, 0, level + 1))
    keep, send, r2, r3 = call(
        path_last,
        (shape(2, 56, LANES), shape(2, 56, LANES), shape(4, LANES), shape(8, LANES)),
        [pltpu.VMEM((SPECIES * PATH, LANES), f32)] + path_scratch(3),
        (*second, x.astype(jnp.int32).reshape(1), places, *waiting, path),
        far=PARTS,
        scalar=(PARTS,),
        sems=PARTS,
    )
    keep = keep + moved(send, "x", near_x)
    turned = keep[0] + moved(keep[1], "x", lambda i: i ^ 1)
    r4 = sum_leaf(turned[0:16], 2, 4)

    wide, chain = pltpu.VMEM((ROWS, LANES), f32), pltpu.VMEM((SPACE, LANES), f32)
    named, places = pltpu.VMEM((2, ROWS, LANES), f32), pltpu.VMEM((BLOCKS, REACH), jnp.int32)
    solved = pltpu.VMEM((ROWS, 8), f32)
    y4, r5 = call(
        forward_high,
        (shape(ROWS, 8), shape(32, LANES)),
        [pltpu.VMEM((ROWS, 16 * LANES + REACH), f32), wide, named, places],
        (high, r4, turned[16:48]),
    )
    r5 = sum_leaf(r5, 2, 5)
    partial = call(top, shape(32, LANES), [pltpu.VMEM((ROWS, 32 * LANES), f32), wide], (high, r5))
    known = [sum_leaf(partial, 2, 5)]
    for level, from_rows in ((4, y4), (3, r3)):
        count = COUNT[level]
        partial = call(
            functools.partial(backward_high, level),
            shape(count, LANES),
            [pltpu.VMEM((ROWS, count * LANES + REACH), f32), wide, chain, named, places, solved],
            (high, from_rows, *known),
        )
        known.append(sum_leaf(partial, 2, level))
    last = call(
        backward_low,
        shape(16, LANES),
        [pltpu.VMEM((ROWS, 896 + 3 * REACH), f32), wide, chain, named, places, solved],
        (low, turned[48:56], r2, *known),
    )
    pieces = [last[0:4], last[8:12], last[12:16]]
    for level in (3, 4, 5):
        place = jnp.remainder(z, 2 ** (level - 2)) * 4
        pieces.append(lax.dynamic_slice_in_dim(known[5 - level], place, 4, 0))
    out = jnp.stack(pieces).reshape(6, BLOCKS, BLOCK)
    out = lax.all_to_all(jnp.transpose(out, (1, 0, 2)), PLANE, 0, 0)
    return jnp.transpose(out.reshape(SPECIES, SLOTS, 6, BLOCK), (2, 1, 0, 3)).reshape(6, BLOCKS, BLOCK)


def solution(mesh):
    cut = Mesh(mesh.devices.reshape(8, 4, 8), ("z", "x", "blk"))
    rows = ("z", "x", "blk")
    placed = (P(None, None, rows), P(rows, None), P(None, rows, None), P(None, rows, None))
    return jax.shard_map(
        local, mesh=cut, in_specs=placed, out_specs=P(None, None, rows), check_vma=False
    )
```

```python
import functools

import jax
import jax.numpy as jnp
from jax import lax
from jax.experimental import pallas as pl
from jax.experimental.pallas import tpu as pltpu
from jax.sharding import Mesh
from jax.sharding import PartitionSpec as P

PLANE = ("x", "blk")
LANES = 128
BLOCK = 16
BLOCKS = 32
ROWS = BLOCK * BLOCKS
REACH = 512
SLOTS = 8
OWN = SLOTS * BLOCK
SPECIES = 4
FIRST = (0, 8, 12, 16, 24, 40)
COUNT = (4, 4, 4, 8, 16, 32)
SPACE = 72
PATH = 64
PARTS = (10, 10, 10, 8, 8)
RHS_AT = 0
NAMED_AT = 256
DIAG_AT = (512, 1152, 1920, 2944, 4480)
OFF_AT = (640, 1408, 2432, 3968, 6528)
CUT = 2944
GROUP = 7040
LEVEL_AT = ((0, 1152), (1152, 1920), (1920, 2944), (2944, 4480), (4480, 7040))
PLANE_DIAG_AT = (0, 128, 384, 896, 1920, 3968)
PLANE_OFF_AT = (8064, 8576, 9088, 9600, 10112)
PLANE_NAMED_AT = 10624
WHOLE = 10880
MIB = 1024 * 1024


def store_named(rows_index, to, at):
    for level in range(5):
        for k in range(2):
            named = rows_index[level, :, k * 256 : (k + 1) * 256].astype(jnp.float32)
            to[2 * level + k : 2 * level + k + 1, at : at + 256] = named
    to[10:16, at : at + 256] = jnp.zeros((6, 256), jnp.float32)


def start_all(moves, sems):
    copies = [pltpu.make_async_copy(source, target, sems.at[k]) for k, (source, target) in enumerate(moves)]
    for copy in copies:
        copy.start()
    return copies


def pack_all(rhs, rows_index, diag_inverse, off_diagonal, pack, first, second, sems):
    moves = []
    for level in range(5):
        part, less = (first, 0) if level < 3 else (second, CUT)
        columns = 2**level * LANES
        diag_at, off_at = DIAG_AT[level] - less, OFF_AT[level] - less
        diag = diag_inverse.at[:, columns - LANES : 2 * columns - LANES]
        moves.append((diag, part.at[:, diag_at : diag_at + columns]))
        moves.append((off_diagonal.at[level], part.at[:, off_at : off_at + REACH]))
    moves.append((diag_inverse, pack.at[:, 0:8064]))
    for level in range(5):
        at = PLANE_OFF_AT[level]
        moves.append((off_diagonal.at[level], pack.at[:, at : at + REACH]))
    copies = start_all(moves, sems)
    given = [rhs[level] for level in range(6)] + [jnp.zeros((BLOCK, 64), jnp.float32)]
    first[:, RHS_AT : RHS_AT + 256] = jnp.concatenate(given, axis=1)
    store_named(rows_index, first, NAMED_AT)
    store_named(rows_index, pack, PLANE_NAMED_AT)
    for copy in copies:
        copy.wait()


def matvec(diag, at, groups, chunks, read_row, write, rows=ROWS):
    size = rows // groups
    for k in range(groups):
        for start in range(k * size, (k + 1) * size, 64):
            total = None
            for c in range(chunks):
                term = diag[start : start + 64, at + c * LANES : at + (c + 1) * LANES] * read_row(k * chunks + c)
                total = term if total is None else total + term
            write(start, jnp.sum(total, axis=1, keepdims=True))


def matvec_transposed(diag, at, groups, chunks, wide, write, rows=ROWS):
    size = rows // groups
    for k in range(groups):
        for c in range(chunks):
            total = None
            for start in range(k * size, (k + 1) * size, 64):
                term = diag[start : start + 64, at + c * LANES : at + (c + 1) * LANES] * wide[start : start + 64, :]
                total = term if total is None else total + term
            write(k * chunks + c, jnp.sum(total, axis=0, keepdims=True))


def split(value):
    coarse = value.astype(jnp.bfloat16)
    return coarse, (value - coarse.astype(jnp.float32)).astype(jnp.bfloat16)


def rows_iota(rows, first):
    return lax.broadcasted_iota(jnp.int32, (rows, REACH), 0) + first


def small(whole):
    return whole.astype(jnp.float32).astype(jnp.bfloat16)


def pick(hit, value):
    return jnp.where(hit, value, jnp.zeros((), jnp.bfloat16))


def lane_one_hot(where, lanes):
    return pick(lanes == small(jnp.bitwise_and(where, 127)), jnp.ones((), jnp.bfloat16))


def block_rows(d):
    return pl.ds(pl.multiple_of(d * BLOCK, BLOCK), BLOCK)


def couple(off, at, chain, place, first, wide):
    height = SPACE - first
    table = jnp.concatenate(split(chain[first:SPACE, :]), axis=0)
    names, lanes = rows_iota(height, first), small(rows_iota(LANES, 0))

    def step(d, carry):
        where = place[pl.ds(d, 1), :]
        rows = jnp.dot(table, lane_one_hot(where, lanes), preferred_element_type=jnp.float32)
        hit = names == jnp.right_shift(where, 7)
        known = jnp.sum(jnp.where(hit, rows[:height] + rows[height:], 0.0), axis=0, keepdims=True)
        drop = jnp.sum(off[block_rows(d), at : at + REACH] * known, axis=1, keepdims=True)
        wide[block_rows(d), :] = jnp.broadcast_to(-drop, (BLOCK, LANES))
        return carry

    lax.fori_loop(0, BLOCKS, step, 0, unroll=BLOCKS)


def fetch(pack, held, sems, cuts):
    copies = []
    for k, (first, last, to) in enumerate(cuts):
        copies.append(
            pltpu.make_async_copy(pack.at[:, first:last], held.at[:, to : to + last - first], sems.at[k])
        )
        copies[-1].start()
    return copies


def fetch_named(pack, named, sems, at):
    first = PLANE_NAMED_AT
    copies = [
        pltpu.make_async_copy(pack.at[:, first + k * LANES : first + (k + 1) * LANES], named.at[k], sems.at[at + k])
        for k in range(2)
    ]
    for copy in copies:
        copy.start()
    return copies


def chain_position(named, level, blocks):
    quarters = [
        named.at[a][pl.ds(2 * level + k, blocks, stride=BLOCK), :] for k in range(2) for a in range(2)
    ]
    return jnp.concatenate(quarters, axis=1).astype(jnp.int32) + (2 ** (level + 1) - 1) * LANES


def find_places(named, level, places):
    chain = chain_position(named, level, BLOCKS)
    if level == 0:
        block = lax.broadcasted_iota(jnp.int32, (BLOCKS, REACH), 0)
        places[...] = chain + jnp.where((chain < 3 * LANES) & (block < 16), 7 * LANES, 9 * LANES)
    else:
        places[...] = chain + 9 * LANES


def fetch_parts(parts, level, held, sems):
    first, last = LEVEL_AT[level]
    less = 0 if level < 3 else CUT
    copies, at = [], 0
    for k, part in enumerate(parts):
        count = part.shape[0]
        copies.append(
            pltpu.make_async_copy(part.at[:, first - less : last - less], held.at[pl.ds(at, count), :], sems.at[k])
        )
        copies[-1].start()
        at += count
    return copies


def path_solve(level, read, held, place, wide, total):
    diag_at, off_at = DIAG_AT[level] - LEVEL_AT[level][0], OFF_AT[level] - LEVEL_AT[level][0]
    for n in range(SPECIES):

        def write(at, value, n=n):
            wide[n, at : at + 64, :] = jnp.broadcast_to(value, (64, LANES))

        matvec(held, diag_at, 1, 2**level, functools.partial(read, n), write, OWN)
    names, lanes = small(rows_iota(PATH, 0)), small(rows_iota(LANES, 0))
    for d in range(SLOTS):
        where = place[d : d + 1, :]
        hit = names == small(jnp.right_shift(where, 7))
        right = lane_one_hot(where, lanes)
        rows = slice(d * BLOCK, (d + 1) * BLOCK)
        left = []
        for n in range(SPECIES):
            solved = jnp.concatenate([wide[n, rows, :]] * (REACH // LANES), axis=1)
            update = jnp.sum(held[rows, off_at : off_at + REACH] * solved, axis=0, keepdims=True)
            left += [pick(hit, part) for part in split(update)]
        product = lax.dot_general(
            jnp.concatenate(left, axis=0), right, (((1,), (1,)), ((), ())), preferred_element_type=jnp.float32
        )
        total[...] = product if d == 0 else total[...] + product


def path_update(level, before, total, path, ahead):
    count = 2 ** (level + 1)
    for n in range(SPECIES):
        at = 2 * n * PATH
        path[n * PATH : (n + 1) * PATH, :] = before[n * PATH : (n + 1) * PATH, :] - (
            total[at : at + PATH, :] + total[at + PATH : at + 2 * PATH, :]
        )
        if ahead is not None:
            ahead[n * count : (n + 1) * count, :] = path[n * PATH + count : n * PATH + 2 * count, :]


def path_first(*refs):
    parts = refs[: PARTS[0]]
    here, path, ahead, r0, places, held, named, turned, wide, total, sems = refs[PARTS[0] :]
    leaf, b = here[0], here[1]
    copies = fetch_parts(parts, 0, held, sems)
    path[...] = jnp.zeros((SPECIES * PATH, LANES), jnp.float32)
    lane = lax.broadcasted_iota(jnp.int32, (BLOCK, LANES), 1)
    row = lax.broadcasted_iota(jnp.int32, (BLOCK, LANES), 0)
    stands = []
    for core in (0, 1):
        for ahead_by in (0, 6, 2, 4):
            slot = jnp.bitwise_and(b + ahead_by, 7) ^ core
            stands.append(jnp.where(lane == row + slot * BLOCK, 1.0, 0.0).astype(jnp.bfloat16))
    order = jnp.concatenate(stands, axis=0)
    for copy in copies:
        copy.wait()
    flipped = jnp.transpose(held[:, RHS_AT : RHS_AT + 256])
    total_rows = None
    for _ in range(3):
        piece = flipped.astype(jnp.bfloat16)
        flipped = flipped - piece.astype(jnp.float32)
        rows = jnp.dot(piece, order, preferred_element_type=jnp.float32)
        total_rows = rows if total_rows is None else total_rows + rows
    turned[...] = total_rows
    for n in range(SPECIES):
        r0[n : n + 1, :] = turned[pl.ds(b * SPECIES + n, 1), :]
        for level in range(1, 6):
            at = n * PATH + 2**level + jnp.bitwise_and(leaf, 2**level - 1)
            path[pl.ds(at, 1), :] = turned[pl.ds(level * 32 + b * SPECIES + n, 1), :]
    for k in range(2):
        named[k] = held[:, NAMED_AT + k * LANES : NAMED_AT + (k + 1) * LANES]
    for level in range(5):
        places[level] = chain_position(named, level, SLOTS) + LANES
    path_solve(0, lambda n, c: r0[n : n + 1, :], held, places.at[0], wide, total)
    path_update(0, path, total, path, ahead)


def path_next(level, *refs):
    parts = refs[: PARTS[level]]
    places, summed, before, path, ahead, held, wide, total, sems = refs[PARTS[level] :]
    copies = fetch_parts(parts, level, held, sems)
    count = 2**level
    for copy in copies:
        copy.wait()
    path_solve(
        level, lambda n, c: summed[n * count + c : n * count + c + 1, :], held, places.at[level], wide, total
    )
    path_update(level, before, total, path, ahead)


def path_last(*refs):
    parts, (place, places, r0, r1, r2, r3, summed, before, keep, send, t2, t3, t4, path, *scratch) = (
        refs[: PARTS[4]], refs[PARTS[4] :]
    )
    path_next(4, *parts, places, summed, before, path, None, *scratch)
    x = place[0]
    even = 1.0 - (x & 1).astype(jnp.float32)
    for n in range(SPECIES):
        slot = n ^ x
        slot = slot ^ (slot >> 1)
        value = jnp.zeros((8, LANES), jnp.float32)
        row = lax.broadcasted_iota(jnp.int32, (8, LANES), 0)
        value = jnp.where(row == x, r0[n : n + 1, :], value)
        for k in range(2):
            value = jnp.where(row == 4 + 2 * (x >> 1) + k, r1[2 * n + k : 2 * n + k + 1, :] * even, value)
        for to, low in ((keep, 0), (send, 2)):

            @pl.when((slot >= low) & (slot < low + 2))
            def _(n=n, slot=slot, value=value, to=to, low=low):
                to[slot - low, 0:32, :] = path[n * PATH + 32 : (n + 1) * PATH, :]
                to[slot - low, 32:40, :] = value

    t2[...] = r2[pl.ds(x * 4, 4), :]
    t3[...] = r3[pl.ds(pl.multiple_of(x * 8, 8), 8), :]
    t4[...] = summed[pl.ds(pl.multiple_of(x * 16, 16), 16), :]


def high_cuts(level):
    columns = COUNT[level] * LANES
    return [
        (PLANE_DIAG_AT[level], PLANE_DIAG_AT[level] + columns, 0),
        (PLANE_OFF_AT[level], PLANE_OFF_AT[level] + REACH, columns),
    ]


def top(pack, summed, partial, held, wide, sems):
    pieces = 8
    size = ROWS // pieces
    copies = []
    for k in range(pieces):
        rows = pl.ds(k * size, size)
        copies.append(
            pltpu.make_async_copy(
                pack.at[rows, PLANE_DIAG_AT[5] : PLANE_DIAG_AT[5] + 32 * LANES], held.at[rows, :], sems.at[k]
            )
        )
        copies[-1].start()
    for k in range(pieces):
        copies[k].wait()
        rows = slice(k * size, (k + 1) * size)

        def write(at, value, k=k):
            wide[k * size + at : k * size + at + 64, :] = jnp.broadcast_to(value, (64, LANES))

        matvec(held.at[rows, :], 0, 1, COUNT[5], lambda c: summed[c : c + 1, :], write, size)

        def write_row(c, value, k=k):
            partial[c : c + 1, :] = value if k == 0 else partial[c : c + 1, :] + value

        matvec_transposed(held.at[rows, :], 0, 1, COUNT[5], wide.at[rows, :], write_row, size)


def backward_high(level, pack, residual, *rest):
    above = rest[: 5 - level]
    partial, held, wide, chain, named, places, sems = rest[5 - level :]
    columns = COUNT[level] * LANES
    named_copies = fetch_named(pack, named, sems, 6)
    copies = fetch(pack, held, sems, high_cuts(level)[::-1])
    for k, value in enumerate(above):
        chain[FIRST[5 - k] : FIRST[5 - k] + COUNT[5 - k], :] = value[...]
    for copy in named_copies:
        copy.wait()
    find_places(named, level, places)
    copies[0].wait()
    couple(held, columns, chain, places, FIRST[level + 1], wide)
    copies[1].wait()

    def write(at, value):
        wide[at : at + 64, :] = wide[at : at + 64, :] + value

    matvec(held, 0, 1, COUNT[level], lambda c: residual[c : c + 1, :], write)

    def write_row(c, value):
        partial[c : c + 1, :] = value

    matvec_transposed(held, 0, 1, COUNT[level], wide, write_row)


def backward_low(pack, r01, r2, s5, s4, s3, out, held, wide, chain, named, places, sems):
    named_copies = fetch_named(pack, named, sems, 6)
    cuts = []
    for level in (2, 1, 0):
        diag_at, off_at = PLANE_DIAG_AT[level], PLANE_OFF_AT[level]
        cuts.append((off_at, off_at + REACH, 896 + REACH * level))
        cuts.append((diag_at, diag_at + LANES * 2**level, LANES * (2**level - 1)))
    copies = fetch(pack, held, sems, cuts)
    for level, value in ((5, s5), (4, s4), (3, s3)):
        chain[FIRST[level] : FIRST[level] + COUNT[level], :] = value[...]
    chain[0:16, :] = jnp.zeros((16, LANES), jnp.float32)
    for copy in named_copies:
        copy.wait()
    for k, level in enumerate((2, 1, 0)):
        find_places(named, level, places)
        copies[2 * k].wait()
        couple(held, 896 + REACH * level, chain, places, 8, wide)

        def write(at, value):
            wide[at : at + 64, :] = wide[at : at + 64, :] + value

        def read(c, level=level):
            return r2[c : c + 1, :] if level == 2 else r01[4 * level + c : 4 * level + c + 1, :]

        copies[2 * k + 1].wait()
        matvec(held, LANES * (2**level - 1), 4 >> level, 1 << level, read, write)

        def write_row(c, value, first=FIRST[level]):
            chain[first + c : first + c + 1, :] = value

        matvec_transposed(held, LANES * (2**level - 1), 4 >> level, 1 << level, wide, write_row)
    out[...] = chain[0:16, :]


def call(body, outs, scratch, args, far=1, scalar=(), sems=8):
    vmem = pl.BlockSpec(memory_space=pltpu.VMEM)
    smem = pl.BlockSpec(memory_space=pltpu.SMEM)
    hbm = pl.BlockSpec(memory_space=pltpu.HBM)
    specs = [hbm if k < far else smem if k in scalar else vmem for k in range(len(args))]
    return pl.pallas_call(
        body,
        out_shape=outs,
        in_specs=specs,
        out_specs=jax.tree.map(lambda _: vmem, outs),
        scratch_shapes=scratch + [pltpu.SemaphoreType.DMA((sems,))],
        compiler_params=pltpu.CompilerParams(vmem_limit_bytes=(52 if far == 1 else 6) * MIB),
        cost_estimate=pl.CostEstimate(flops=2**29, bytes_accessed=2**20, transcendentals=0),
    )(*args)


def shape(*dims, kind=jnp.float32):
    return jax.ShapeDtypeStruct(dims, kind)


def moved(value, axis, to):
    size = lax.axis_size(axis)
    return lax.ppermute(value, axis, [(i, to(i)) for i in range(size)])


def near_x(i):
    return 3 - i


def far_z(i):
    return (i + 5) % 8 if i % 2 else (i + 3) % 8


def sum_leaf(value, first, last):
    steps = [("x", lambda i: i ^ 1), ("x", near_x), ("z", lambda i: i ^ 1)]
    if last < 5:
        steps.append(("z", lambda i: i ^ 2))
    else:
        steps.append(("z", lambda i: (i + 1) % 8 if i % 2 else (i + 7) % 8))
        steps.append(("z", far_z))
    for axis, to in steps[first:last]:
        value = value + moved(value, axis, to)
    return value


def local(rhs, diag_inverse, off_diagonal, rows_index):
    f32 = jnp.float32
    x, z = lax.axis_index("x"), lax.axis_index("z")
    leaf = z * 4 + x
    hbm, vmem = pl.BlockSpec(memory_space=pltpu.HBM), pl.BlockSpec(memory_space=pltpu.VMEM)
    pack, first, second = pl.pallas_call(
        pack_all,
        out_shape=(shape(BLOCK, WHOLE), shape(BLOCK, CUT), shape(BLOCK, GROUP - CUT)),
        in_specs=[vmem, vmem, hbm, hbm],
        out_specs=(vmem,) * 3,
        scratch_shapes=[pltpu.SemaphoreType.DMA((16,))],
        compiler_params=pltpu.CompilerParams(vmem_limit_bytes=6 * MIB),
    )(jnp.transpose(rhs, (0, 2, 1)), rows_index, diag_inverse, off_diagonal)
    pack = lax.all_gather(pack, PLANE, axis=0, tiled=True)

    def other_core(parts):
        return parts + tuple(moved(part, "blk", lambda i: i ^ 1) for part in parts)

    half = BLOCK // 2
    down, up = (moved(first, "blk", lambda i, hop=hop: (i + hop) % SLOTS) for hop in (2, 6))
    across = (
        moved(down[:half], "blk", lambda i: (i + 2) % SLOTS),
        moved(up[half:], "blk", lambda i: (i + 6) % SLOTS),
    )
    first = other_core((first, down, up, *across))
    second = lax.optimization_barrier((second, first[-1]))[0]
    second = (second,) + tuple(moved(second, "blk", lambda i, hop=hop: (i + hop) % SLOTS) for hop in (2, 6, 4))

    def path_scratch(level, *more):
        return [
            pltpu.VMEM((OWN, LEVEL_AT[level][1] - LEVEL_AT[level][0]), f32),
            *more,
            pltpu.VMEM((SPECIES, OWN, LANES), f32),
            pltpu.VMEM((SPECIES * 2 * PATH, LANES), f32),
        ]

    here = jnp.stack([leaf, lax.axis_index("blk")]).astype(jnp.int32)
    path, ahead, r0, places = call(
        path_first,
        (
            shape(SPECIES * PATH, LANES), shape(SPECIES * 2, LANES), shape(SPECIES, LANES),
            shape(5, SLOTS, REACH, kind=jnp.int32),
        ),
        path_scratch(0, pltpu.VMEM((2, OWN, LANES), f32), pltpu.VMEM((256, LANES), f32)),
        (*first, here),
        far=PARTS[0],
        scalar=(PARTS[0],),
        sems=PARTS[0],
    )
    waiting = [r0, sum_leaf(ahead, 0, 1)]
    for level in (1, 2, 3):
        path, ahead = call(
            functools.partial(path_next, level),
            (shape(SPECIES * PATH, LANES), shape(SPECIES * 2 ** (level + 1), LANES)),
            path_scratch(level),
            (*(first if level < 3 else second), places, waiting[level], path),
            far=PARTS[level],
            sems=PARTS[level],
        )
        if level == 2:
            second = other_core(lax.optimization_barrier((*second, ahead))[:4])
        waiting.append(sum_leaf(ahead, 0, level + 1))
    keep, send, r2, r3, r4 = call(
        path_last,
        (shape(2, 40, LANES), shape(2, 40, LANES), shape(4, LANES), shape(8, LANES), shape(16, LANES)),
        [pltpu.VMEM((SPECIES * PATH, LANES), f32)] + path_scratch(4),
        (*second, x.astype(jnp.int32).reshape(1), places, *waiting, path),
        far=PARTS[4],
        scalar=(PARTS[4],),
        sems=PARTS[4],
    )
    keep = keep + moved(send, "x", near_x)
    turned = keep[0] + moved(keep[1], "x", lambda i: i ^ 1)
    r5 = sum_leaf(turned[0:32], 2, 5)

    wide, chain = pltpu.VMEM((ROWS, LANES), f32), pltpu.VMEM((SPACE, LANES), f32)
    named, places = pltpu.VMEM((2, ROWS, LANES), f32), pltpu.VMEM((BLOCKS, REACH), jnp.int32)
    partial = call(top, shape(32, LANES), [pltpu.VMEM((ROWS, 32 * LANES), f32), wide], (pack, r5))
    known = [sum_leaf(partial, 2, 5)]
    for level, from_rows in ((4, r4), (3, r3)):
        count = COUNT[level]
        partial = call(
            functools.partial(backward_high, level),
            shape(count, LANES),
            [pltpu.VMEM((ROWS, count * LANES + REACH), f32), wide, chain, named, places],
            (pack, from_rows, *known),
        )
        known.append(sum_leaf(partial, 2, level))
    last = call(
        backward_low,
        shape(16, LANES),
        [pltpu.VMEM((ROWS, 896 + 3 * REACH), f32), wide, chain, named, places],
        (pack, turned[32:40], r2, *known),
    )
    pieces = [last[0:4], last[8:12], last[12:16]]
    for level in (3, 4, 5):
        place = jnp.remainder(z, 2 ** (level - 2)) * 4
        pieces.append(lax.dynamic_slice_in_dim(known[5 - level], place, 4, 0))
    out = jnp.stack(pieces).reshape(6, BLOCKS, BLOCK)
    out = lax.all_to_all(jnp.transpose(out, (1, 0, 2)), PLANE, 0, 0)
    return jnp.transpose(out.reshape(SPECIES, SLOTS, 6, BLOCK), (2, 1, 0, 3)).reshape(6, BLOCKS, BLOCK)


def solution(mesh):
    cut = Mesh(mesh.devices.reshape(8, 4, 8), ("z", "x", "blk"))
    rows = ("z", "x", "blk")
    placed = (P(None, None, rows), P(rows, None), P(None, rows, None), P(None, rows, None))
    return jax.shard_map(
        local, mesh=cut, in_specs=placed, out_specs=P(None, None, rows), check_vma=False
    )
```

```python
import functools

import jax
import jax.numpy as jnp
from jax import lax
from jax.experimental import pallas as pl
from jax.experimental.pallas import tpu as pltpu
from jax.sharding import Mesh
from jax.sharding import PartitionSpec as P

PLANE = ("x", "blk")
LANES = 128
BLOCK = 16
BLOCKS = 32
ROWS = BLOCK * BLOCKS
REACH = 512
SLOTS = 8
OWN = SLOTS * BLOCK
SPECIES = 4
FIRST = (0, 8, 12, 16, 24, 40)
COUNT = (4, 4, 4, 8, 16, 32)
SPACE = 72
PATH = 64
PARTS = (10, 10, 10, 8, 8)
RHS_AT = 0
NAMED_AT = 256
DIAG_AT = (512, 1152, 1920, 2944, 4480)
OFF_AT = (640, 1408, 2432, 3968, 6528)
CUT = 2944
GROUP = 7040
LEVEL_AT = ((0, 1152), (1152, 1920), (1920, 2944), (2944, 4480), (4480, 7040))
PLANE_DIAG_AT = (0, 128, 384, 896, 1920, 3968)
PLANE_OFF_AT = (8064, 8576, 9088, 9600, 10112)
PLANE_NAMED_AT = 10624
WHOLE = 10880
MIB = 1024 * 1024


def store_named(rows_index, to, at):
    for level in range(5):
        for k in range(2):
            named = rows_index[level, :, k * 256 : (k + 1) * 256].astype(jnp.float32)
            to[2 * level + k : 2 * level + k + 1, at : at + 256] = named
    to[10:16, at : at + 256] = jnp.zeros((6, 256), jnp.float32)


def start_all(moves, sems):
    copies = [pltpu.make_async_copy(source, target, sems.at[k]) for k, (source, target) in enumerate(moves)]
    for copy in copies:
        copy.start()
    return copies


def pack_all(rhs, rows_index, diag_inverse, off_diagonal, pack, first, second, sems):
    moves = []
    for level in range(5):
        part, less = (first, 0) if level < 3 else (second, CUT)
        columns = 2**level * LANES
        diag_at, off_at = DIAG_AT[level] - less, OFF_AT[level] - less
        diag = diag_inverse.at[:, columns - LANES : 2 * columns - LANES]
        moves.append((diag, part.at[:, diag_at : diag_at + columns]))
        moves.append((off_diagonal.at[level], part.at[:, off_at : off_at + REACH]))
    moves.append((diag_inverse, pack.at[:, 0:8064]))
    for level in range(5):
        at = PLANE_OFF_AT[level]
        moves.append((off_diagonal.at[level], pack.at[:, at : at + REACH]))
    copies = start_all(moves, sems)
    given = [rhs[level] for level in range(6)] + [jnp.zeros((BLOCK, 64), jnp.float32)]
    first[:, RHS_AT : RHS_AT + 256] = jnp.concatenate(given, axis=1)
    store_named(rows_index, first, NAMED_AT)
    store_named(rows_index, pack, PLANE_NAMED_AT)
    for copy in copies:
        copy.wait()


def matvec(diag, at, groups, chunks, read_row, write, rows=ROWS):
    size = rows // groups

    def step(k, start):
        total = None
        for c in range(chunks):
            term = diag[pl.ds(start, 64), at + c * LANES : at + (c + 1) * LANES] * read_row(k * chunks + c)
            total = term if total is None else total + term
        write(start, jnp.sum(total, axis=1, keepdims=True))

    for k in range(groups):
        for start in range(k * size, (k + 1) * size, 64):
            step(k, start)


def matvec_transposed(diag, at, groups, chunks, wide, write, rows=ROWS):
    size = rows // groups

    def step(k, c):
        total = None
        for start in range(k * size, (k + 1) * size, 64):
            columns = pl.ds(at + c * LANES, LANES) if isinstance(c, int) else pl.ds(pl.multiple_of(at + c * LANES, LANES), LANES)
            term = diag[start : start + 64, columns] * wide[start : start + 64, :]
            total = term if total is None else total + term
        write(k * chunks + c, jnp.sum(total, axis=0, keepdims=True))

    for k in range(groups):
        for c in range(chunks):
            step(k, c)


def split(value):
    coarse = value.astype(jnp.bfloat16)
    return coarse, (value - coarse.astype(jnp.float32)).astype(jnp.bfloat16)


def rows_iota(rows, first):
    return lax.broadcasted_iota(jnp.int32, (rows, REACH), 0) + first


def small(whole):
    return whole.astype(jnp.float32).astype(jnp.bfloat16)


def pick(hit, value):
    return jnp.where(hit, value, jnp.zeros((), jnp.bfloat16))


def lane_one_hot(where, lanes):
    return pick(lanes == small(jnp.bitwise_and(where, 127)), jnp.ones((), jnp.bfloat16))


def block_rows(d):
    return pl.ds(pl.multiple_of(d * BLOCK, BLOCK), BLOCK)


def couple(off, at, chain, place, first, wide):
    height = SPACE - first
    table = jnp.concatenate(split(chain[first:SPACE, :]), axis=0)
    names, lanes = rows_iota(height, first), small(rows_iota(LANES, 0))

    def step(d, carry):
        where = place[pl.ds(d, 1), :]
        rows = jnp.dot(table, lane_one_hot(where, lanes), preferred_element_type=jnp.float32)
        hit = names == jnp.right_shift(where, 7)
        known = jnp.sum(jnp.where(hit, rows[:height] + rows[height:], 0.0), axis=0, keepdims=True)
        drop = jnp.sum(off[block_rows(d), at : at + REACH] * known, axis=1, keepdims=True)
        wide[block_rows(d), :] = jnp.broadcast_to(-drop, (BLOCK, LANES))
        return carry

    lax.fori_loop(0, BLOCKS, step, 0, unroll=16)


def fetch(pack, held, sems, cuts):
    copies = []
    for k, (first, last, to) in enumerate(cuts):
        copies.append(
            pltpu.make_async_copy(pack.at[:, first:last], held.at[:, to : to + last - first], sems.at[k])
        )
        copies[-1].start()
    return copies


def fetch_named(pack, named, sems, at):
    first = PLANE_NAMED_AT
    copies = [
        pltpu.make_async_copy(pack.at[:, first + k * LANES : first + (k + 1) * LANES], named.at[k], sems.at[at + k])
        for k in range(2)
    ]
    for copy in copies:
        copy.start()
    return copies


def chain_position(named, level, blocks):
    quarters = [
        named.at[a][pl.ds(2 * level + k, blocks, stride=BLOCK), :] for k in range(2) for a in range(2)
    ]
    return jnp.concatenate(quarters, axis=1).astype(jnp.int32) + (2 ** (level + 1) - 1) * LANES


def find_places(named, level, places):
    chain = chain_position(named, level, BLOCKS)
    if level == 0:
        block = lax.broadcasted_iota(jnp.int32, (BLOCKS, REACH), 0)
        places[...] = chain + jnp.where((chain < 3 * LANES) & (block < 16), 7 * LANES, 9 * LANES)
    else:
        places[...] = chain + 9 * LANES


def fetch_parts(parts, level, held, sems):
    first, last = LEVEL_AT[level]
    less = 0 if level < 3 else CUT
    copies, at = [], 0
    for k, part in enumerate(parts):
        count = part.shape[0]
        copies.append(
            pltpu.make_async_copy(part.at[:, first - less : last - less], held.at[pl.ds(at, count), :], sems.at[k])
        )
        copies[-1].start()
        at += count
    return copies


def path_solve(level, read, held, place, wide, total):
    diag_at, off_at = DIAG_AT[level] - LEVEL_AT[level][0], OFF_AT[level] - LEVEL_AT[level][0]
    for n in range(SPECIES):

        def write(at, value, n=n):
            wide[n, at : at + 64, :] = jnp.broadcast_to(value, (64, LANES))

        matvec(held, diag_at, 1, 2**level, functools.partial(read, n), write, OWN)
    names, lanes = small(rows_iota(PATH, 0)), small(rows_iota(LANES, 0))
    total[...] = jnp.zeros_like(total)

    def slot(d, carry):
        where = place[pl.ds(d, 1), :]
        hit = names == small(jnp.right_shift(where, 7))
        right = lane_one_hot(where, lanes)
        rows = block_rows(d)
        left = []
        for n in range(SPECIES):
            solved = jnp.concatenate([wide[n, rows, :]] * (REACH // LANES), axis=1)
            update = jnp.sum(held[rows, off_at : off_at + REACH] * solved, axis=0, keepdims=True)
            left += [pick(hit, part) for part in split(update)]
        total[...] += lax.dot_general(
            jnp.concatenate(left, axis=0), right, (((1,), (1,)), ((), ())), preferred_element_type=jnp.float32
        )
        return carry

    lax.fori_loop(0, SLOTS, slot, 0, unroll=4)


def path_update(level, before, total, path, ahead):
    count = 2 ** (level + 1)
    for n in range(SPECIES):
        at = 2 * n * PATH
        path[n * PATH : (n + 1) * PATH, :] = before[n * PATH : (n + 1) * PATH, :] - (
            total[at : at + PATH, :] + total[at + PATH : at + 2 * PATH, :]
        )
        if ahead is not None:
            ahead[n * count : (n + 1) * count, :] = path[n * PATH + count : n * PATH + 2 * count, :]


def path_first(*refs):
    parts = refs[: PARTS[0]]
    here, path, ahead, r0, places, held, named, turned, wide, total, sems = refs[PARTS[0] :]
    leaf, b = here[0], here[1]
    copies = fetch_parts(parts, 0, held, sems)
    path[...] = jnp.zeros((SPECIES * PATH, LANES), jnp.float32)
    lane = lax.broadcasted_iota(jnp.int32, (BLOCK, LANES), 1)
    row = lax.broadcasted_iota(jnp.int32, (BLOCK, LANES), 0)
    stands = []
    for core in (0, 1):
        for ahead_by in (0, 6, 2, 4):
            slot = jnp.bitwise_and(b + ahead_by, 7) ^ core
            stands.append(jnp.where(lane == row + slot * BLOCK, 1.0, 0.0).astype(jnp.bfloat16))
    order = jnp.concatenate(stands, axis=0)
    for copy in copies:
        copy.wait()
    flipped = jnp.transpose(held[:, RHS_AT : RHS_AT + 256])
    total_rows = None
    for _ in range(3):
        piece = flipped.astype(jnp.bfloat16)
        flipped = flipped - piece.astype(jnp.float32)
        rows = jnp.dot(piece, order, preferred_element_type=jnp.float32)
        total_rows = rows if total_rows is None else total_rows + rows
    turned[...] = total_rows
    for n in range(SPECIES):
        r0[n : n + 1, :] = turned[pl.ds(b * SPECIES + n, 1), :]
        for level in range(1, 6):
            at = n * PATH + 2**level + jnp.bitwise_and(leaf, 2**level - 1)
            path[pl.ds(at, 1), :] = turned[pl.ds(level * 32 + b * SPECIES + n, 1), :]
    for k in range(2):
        named[k] = held[:, NAMED_AT + k * LANES : NAMED_AT + (k + 1) * LANES]
    for level in range(5):
        places[level] = chain_position(named, level, SLOTS) + LANES
    path_solve(0, lambda n, c: r0[n : n + 1, :], held, places.at[0], wide, total)
    path_update(0, path, total, path, ahead)


def path_next(level, *refs):
    parts = refs[: PARTS[level]]
    places, summed, before, path, ahead, held, wide, total, sems = refs[PARTS[level] :]
    copies = fetch_parts(parts, level, held, sems)
    count = 2**level
    for copy in copies:
        copy.wait()
    path_solve(
        level, lambda n, c: summed[n * count + c : n * count + c + 1, :], held, places.at[level], wide, total
    )
    path_update(level, before, total, path, ahead)


def path_last(*refs):
    parts, (place, places, r0, r1, r2, r3, summed, before, keep, send, t2, t3, t4, path, *scratch) = (
        refs[: PARTS[4]], refs[PARTS[4] :]
    )
    path_next(4, *parts, places, summed, before, path, None, *scratch)
    x = place[0]
    even = 1.0 - (x & 1).astype(jnp.float32)
    for n in range(SPECIES):
        slot = n ^ x
        slot = slot ^ (slot >> 1)
        value = jnp.zeros((8, LANES), jnp.float32)
        row = lax.broadcasted_iota(jnp.int32, (8, LANES), 0)
        value = jnp.where(row == x, r0[n : n + 1, :], value)
        for k in range(2):
            value = jnp.where(row == 4 + 2 * (x >> 1) + k, r1[2 * n + k : 2 * n + k + 1, :] * even, value)
        for to, low in ((keep, 0), (send, 2)):

            @pl.when((slot >= low) & (slot < low + 2))
            def _(n=n, slot=slot, value=value, to=to, low=low):
                to[slot - low, 0:32, :] = path[n * PATH + 32 : (n + 1) * PATH, :]
                to[slot - low, 32:40, :] = value

    t2[...] = r2[pl.ds(x * 4, 4), :]
    t3[...] = r3[pl.ds(pl.multiple_of(x * 8, 8), 8), :]
    t4[...] = summed[pl.ds(pl.multiple_of(x * 16, 16), 16), :]


def high_cuts(level):
    columns = COUNT[level] * LANES
    return [
        (PLANE_DIAG_AT[level], PLANE_DIAG_AT[level] + columns, 0),
        (PLANE_OFF_AT[level], PLANE_OFF_AT[level] + REACH, columns),
    ]


def top(pack, summed, partial, held, wide, sems):
    pieces = 8
    size = ROWS // pieces

    def piece(k):
        rows = pl.ds(pl.multiple_of(k * size, size), size)
        columns = pl.ds(PLANE_DIAG_AT[5], COUNT[5] * LANES)
        return rows, pltpu.make_async_copy(pack.at[rows, columns], held.at[rows, :], sems.at[k])

    for k in range(pieces):
        piece(k)[1].start()
    partial[...] = jnp.zeros((COUNT[5], LANES), jnp.float32)

    @pl.loop(0, pieces)
    def _(k):
        rows, copy = piece(k)
        copy.wait()

        def write(at, value):
            wide[...] = jnp.broadcast_to(value, (size, LANES))

        matvec(held.at[rows, :], 0, 1, COUNT[5], lambda c: summed[c : c + 1, :], write, size)

        def write_row(c, value):
            partial[pl.ds(c, 1), :] = partial[pl.ds(c, 1), :] + value

        for c in range(COUNT[5]):
            term = held[rows, c * LANES : (c + 1) * LANES] * wide[...]
            write_row(c, jnp.sum(term, axis=0, keepdims=True))


def backward_high(level, pack, residual, *rest):
    above = rest[: 5 - level]
    partial, held, wide, chain, named, places, sems = rest[5 - level :]
    columns = COUNT[level] * LANES
    named_copies = fetch_named(pack, named, sems, 6)
    copies = fetch(pack, held, sems, high_cuts(level)[::-1])
    for k, value in enumerate(above):
        chain[FIRST[5 - k] : FIRST[5 - k] + COUNT[5 - k], :] = value[...]
    for copy in named_copies:
        copy.wait()
    find_places(named, level, places)
    copies[0].wait()
    couple(held, columns, chain, places, FIRST[level + 1], wide)
    copies[1].wait()

    def write(at, value):
        wide[pl.ds(at, 64), :] = wide[pl.ds(at, 64), :] + value

    matvec(held, 0, 1, COUNT[level], lambda c: residual[c : c + 1, :], write)

    def write_row(c, value):
        partial[pl.ds(c, 1), :] = value

    matvec_transposed(held, 0, 1, COUNT[level], wide, write_row)


def backward_low(pack, r01, r2, s5, s4, s3, out, held, wide, chain, named, places, sems):
    named_copies = fetch_named(pack, named, sems, 6)
    cuts = []
    for level in (2, 1, 0):
        diag_at, off_at = PLANE_DIAG_AT[level], PLANE_OFF_AT[level]
        cuts.append((off_at, off_at + REACH, 896 + REACH * level))
        cuts.append((diag_at, diag_at + LANES * 2**level, LANES * (2**level - 1)))
    copies = fetch(pack, held, sems, cuts)
    for level, value in ((5, s5), (4, s4), (3, s3)):
        chain[FIRST[level] : FIRST[level] + COUNT[level], :] = value[...]
    chain[0:16, :] = jnp.zeros((16, LANES), jnp.float32)
    for copy in named_copies:
        copy.wait()
    for k, level in enumerate((2, 1, 0)):
        find_places(named, level, places)
        copies[2 * k].wait()
        couple(held, 896 + REACH * level, chain, places, 8, wide)

        def write(at, value):
            wide[pl.ds(at, 64), :] = wide[pl.ds(at, 64), :] + value

        def read(c, level=level):
            return r2[c : c + 1, :] if level == 2 else r01[4 * level + c : 4 * level + c + 1, :]

        copies[2 * k + 1].wait()
        matvec(held, LANES * (2**level - 1), 4 >> level, 1 << level, read, write)

        def write_row(c, value, first=FIRST[level]):
            chain[first + c : first + c + 1, :] = value

        matvec_transposed(held, LANES * (2**level - 1), 4 >> level, 1 << level, wide, write_row)
    out[...] = chain[0:16, :]


def call(body, outs, scratch, args, far=1, scalar=(), sems=8):
    vmem = pl.BlockSpec(memory_space=pltpu.VMEM)
    smem = pl.BlockSpec(memory_space=pltpu.SMEM)
    hbm = pl.BlockSpec(memory_space=pltpu.HBM)
    specs = [hbm if k < far else smem if k in scalar else vmem for k in range(len(args))]
    return pl.pallas_call(
        body,
        out_shape=outs,
        in_specs=specs,
        out_specs=jax.tree.map(lambda _: vmem, outs),
        scratch_shapes=scratch + [pltpu.SemaphoreType.DMA((sems,))],
        compiler_params=pltpu.CompilerParams(vmem_limit_bytes=(52 if far == 1 else 6) * MIB),
        cost_estimate=pl.CostEstimate(flops=2**29, bytes_accessed=2**20, transcendentals=0),
    )(*args)


def shape(*dims, kind=jnp.float32):
    return jax.ShapeDtypeStruct(dims, kind)


def moved(value, axis, to):
    size = lax.axis_size(axis)
    return lax.ppermute(value, axis, [(i, to(i)) for i in range(size)])


def near_x(i):
    return 3 - i


def far_z(i):
    return (i + 5) % 8 if i % 2 else (i + 3) % 8


def sum_leaf(value, first, last):
    steps = [("x", lambda i: i ^ 1), ("x", near_x), ("z", lambda i: i ^ 1)]
    if last < 5:
        steps.append(("z", lambda i: i ^ 2))
    else:
        steps.append(("z", lambda i: (i + 1) % 8 if i % 2 else (i + 7) % 8))
        steps.append(("z", far_z))
    for axis, to in steps[first:last]:
        value = value + moved(value, axis, to)
    return value


def local(rhs, diag_inverse, off_diagonal, rows_index):
    f32 = jnp.float32
    x, z = lax.axis_index("x"), lax.axis_index("z")
    leaf = z * 4 + x
    hbm, vmem = pl.BlockSpec(memory_space=pltpu.HBM), pl.BlockSpec(memory_space=pltpu.VMEM)
    pack, first, second = pl.pallas_call(
        pack_all,
        out_shape=(shape(BLOCK, WHOLE), shape(BLOCK, CUT), shape(BLOCK, GROUP - CUT)),
        in_specs=[vmem, vmem, hbm, hbm],
        out_specs=(vmem,) * 3,
        scratch_shapes=[pltpu.SemaphoreType.DMA((16,))],
        compiler_params=pltpu.CompilerParams(vmem_limit_bytes=6 * MIB),
    )(jnp.transpose(rhs, (0, 2, 1)), rows_index, diag_inverse, off_diagonal)
    pack = lax.all_gather(pack, PLANE, axis=0, tiled=True)

    def other_core(parts):
        return parts + tuple(moved(part, "blk", lambda i: i ^ 1) for part in parts)

    half = BLOCK // 2
    down, up = (moved(first, "blk", lambda i, hop=hop: (i + hop) % SLOTS) for hop in (2, 6))
    across = (
        moved(down[:half], "blk", lambda i: (i + 2) % SLOTS),
        moved(up[half:], "blk", lambda i: (i + 6) % SLOTS),
    )
    first = other_core((first, down, up, *across))
    second = lax.optimization_barrier((second, first[-1]))[0]
    second = (second,) + tuple(moved(second, "blk", lambda i, hop=hop: (i + hop) % SLOTS) for hop in (2, 6, 4))

    def path_scratch(level, *more):
        return [
            pltpu.VMEM((OWN, LEVEL_AT[level][1] - LEVEL_AT[level][0]), f32),
            *more,
            pltpu.VMEM((SPECIES, OWN, LANES), f32),
            pltpu.VMEM((SPECIES * 2 * PATH, LANES), f32),
        ]

    here = jnp.stack([leaf, lax.axis_index("blk")]).astype(jnp.int32)
    path, ahead, r0, places = call(
        path_first,
        (
            shape(SPECIES * PATH, LANES), shape(SPECIES * 2, LANES), shape(SPECIES, LANES),
            shape(5, SLOTS, REACH, kind=jnp.int32),
        ),
        path_scratch(0, pltpu.VMEM((2, OWN, LANES), f32), pltpu.VMEM((256, LANES), f32)),
        (*first, here),
        far=PARTS[0],
        scalar=(PARTS[0],),
        sems=PARTS[0],
    )
    waiting = [r0, sum_leaf(ahead, 0, 1)]
    for level in (1, 2, 3):
        path, ahead = call(
            functools.partial(path_next, level),
            (shape(SPECIES * PATH, LANES), shape(SPECIES * 2 ** (level + 1), LANES)),
            path_scratch(level),
            (*(first if level < 3 else second), places, waiting[level], path),
            far=PARTS[level],
            sems=PARTS[level],
        )
        if level == 2:
            second = other_core(lax.optimization_barrier((*second, ahead))[:4])
        waiting.append(sum_leaf(ahead, 0, level + 1))
    keep, send, r2, r3, r4 = call(
        path_last,
        (shape(2, 40, LANES), shape(2, 40, LANES), shape(4, LANES), shape(8, LANES), shape(16, LANES)),
        [pltpu.VMEM((SPECIES * PATH, LANES), f32)] + path_scratch(4),
        (*second, x.astype(jnp.int32).reshape(1), places, *waiting, path),
        far=PARTS[4],
        scalar=(PARTS[4],),
        sems=PARTS[4],
    )
    keep = keep + moved(send, "x", near_x)
    turned = keep[0] + moved(keep[1], "x", lambda i: i ^ 1)
    r5 = sum_leaf(turned[0:32], 2, 5)

    wide, chain = pltpu.VMEM((ROWS, LANES), f32), pltpu.VMEM((SPACE, LANES), f32)
    named, places = pltpu.VMEM((2, ROWS, LANES), f32), pltpu.VMEM((BLOCKS, REACH), jnp.int32)
    partial = call(top, shape(32, LANES), [pltpu.VMEM((ROWS, 32 * LANES), f32), pltpu.VMEM((ROWS // 8, LANES), f32)], (pack, r5))
    known = [sum_leaf(partial, 2, 5)]
    for level, from_rows in ((4, r4), (3, r3)):
        count = COUNT[level]
        partial = call(
            functools.partial(backward_high, level),
            shape(count, LANES),
            [pltpu.VMEM((ROWS, count * LANES + REACH), f32), wide, chain, named, places],
            (pack, from_rows, *known),
        )
        known.append(sum_leaf(partial, 2, level))
    last = call(
        backward_low,
        shape(16, LANES),
        [pltpu.VMEM((ROWS, 896 + 3 * REACH), f32), wide, chain, named, places],
        (pack, turned[32:40], r2, *known),
    )
    pieces = [last[0:4], last[8:12], last[12:16]]
    for level in (3, 4, 5):
        place = jnp.remainder(z, 2 ** (level - 2)) * 4
        pieces.append(lax.dynamic_slice_in_dim(known[5 - level], place, 4, 0))
    out = jnp.stack(pieces).reshape(6, BLOCKS, BLOCK)
    out = lax.all_to_all(jnp.transpose(out, (1, 0, 2)), PLANE, 0, 0)
    return jnp.transpose(out.reshape(SPECIES, SLOTS, 6, BLOCK), (2, 1, 0, 3)).reshape(6, BLOCKS, BLOCK)


def solution(mesh):
    cut = Mesh(mesh.devices.reshape(8, 4, 8), ("z", "x", "blk"))
    rows = ("z", "x", "blk")
    placed = (P(None, None, rows), P(rows, None), P(None, rows, None), P(None, rows, None))
    return jax.shard_map(
        local, mesh=cut, in_specs=placed, out_specs=P(None, None, rows), check_vma=False
    )
```

```python
import functools

import jax
import jax.numpy as jnp
from jax import lax
from jax.experimental import pallas as pl
from jax.experimental.pallas import tpu as pltpu
from jax.sharding import Mesh
from jax.sharding import PartitionSpec as P

PLANE = ("x", "blk")
LANES = 128
BLOCK = 16
BLOCKS = 32
ROWS = BLOCK * BLOCKS
REACH = 512
SLOTS = 8
OWN = SLOTS * BLOCK
SPECIES = 4
FIRST = (0, 8, 12, 16, 24, 40)
COUNT = (4, 4, 4, 8, 16, 32)
SPACE = 72
PATH = 64
PARTS = (8, 8, 8, 8, 8)
RHS_AT = 0
NAMED_AT = 256
DIAG_AT = (512, 1152, 1920, 2944, 4480)
OFF_AT = (640, 1408, 2432, 3968, 6528)
CUT = 2944
GROUP = 7040
LEVEL_AT = ((0, 1152), (1152, 1920), (1920, 2944), (2944, 4480), (4480, 7040))
PLANE_DIAG_AT = (0, 128, 384, 896, 1920, 3968)
PLANE_OFF_AT = (8064, 8576, 9088, 9600, 10112)
PLANE_NAMED_AT = 10624
WHOLE = 10880
MIB = 1024 * 1024


def store_named(rows_index, to, at):
    for level in range(5):
        for k in range(2):
            named = rows_index[level, :, k * 256 : (k + 1) * 256].astype(jnp.float32)
            to[2 * level + k : 2 * level + k + 1, at : at + 256] = named
    to[10:16, at : at + 256] = jnp.zeros((6, 256), jnp.float32)


def start_all(moves, sems):
    copies = [pltpu.make_async_copy(source, target, sems.at[k]) for k, (source, target) in enumerate(moves)]
    for copy in copies:
        copy.start()
    return copies


def pack_all(rhs, rows_index, diag_inverse, off_diagonal, pack, first, second, sems):
    moves = []
    for level in range(5):
        part, less = (first, 0) if level < 3 else (second, CUT)
        columns = 2**level * LANES
        diag_at, off_at = DIAG_AT[level] - less, OFF_AT[level] - less
        diag = diag_inverse.at[:, columns - LANES : 2 * columns - LANES]
        moves.append((diag, part.at[:, diag_at : diag_at + columns]))
        moves.append((off_diagonal.at[level], part.at[:, off_at : off_at + REACH]))
    moves.append((diag_inverse, pack.at[:, 0:8064]))
    for level in range(5):
        at = PLANE_OFF_AT[level]
        moves.append((off_diagonal.at[level], pack.at[:, at : at + REACH]))
    copies = start_all(moves, sems)
    given = [rhs[level] for level in range(6)] + [jnp.zeros((BLOCK, 64), jnp.float32)]
    first[:, RHS_AT : RHS_AT + 256] = jnp.concatenate(given, axis=1)
    store_named(rows_index, first, NAMED_AT)
    store_named(rows_index, pack, PLANE_NAMED_AT)
    for copy in copies:
        copy.wait()


def matvec(diag, at, groups, chunks, read_row, write, rows=ROWS):
    size = rows // groups

    def step(k, start):
        total = None
        for c in range(chunks):
            term = diag[pl.ds(start, 64), at + c * LANES : at + (c + 1) * LANES] * read_row(k * chunks + c)
            total = term if total is None else total + term
        write(start, jnp.sum(total, axis=1, keepdims=True))

    for k in range(groups):
        for start in range(k * size, (k + 1) * size, 64):
            step(k, start)


def matvec_transposed(diag, at, groups, chunks, wide, write, rows=ROWS):
    size = rows // groups

    def step(k, c):
        total = None
        for start in range(k * size, (k + 1) * size, 64):
            columns = pl.ds(at + c * LANES, LANES) if isinstance(c, int) else pl.ds(pl.multiple_of(at + c * LANES, LANES), LANES)
            term = diag[start : start + 64, columns] * wide[start : start + 64, :]
            total = term if total is None else total + term
        write(k * chunks + c, jnp.sum(total, axis=0, keepdims=True))

    for k in range(groups):
        for c in range(chunks):
            step(k, c)


def split(value):
    coarse = value.astype(jnp.bfloat16)
    return coarse, (value - coarse.astype(jnp.float32)).astype(jnp.bfloat16)


def rows_iota(rows, first):
    return lax.broadcasted_iota(jnp.int32, (rows, REACH), 0) + first


def small(whole):
    return whole.astype(jnp.float32).astype(jnp.bfloat16)


def pick(hit, value):
    return jnp.where(hit, value, jnp.zeros((), jnp.bfloat16))


def lane_one_hot(where, lanes):
    return pick(lanes == small(jnp.bitwise_and(where, 127)), jnp.ones((), jnp.bfloat16))


def block_rows(d):
    return pl.ds(pl.multiple_of(d * BLOCK, BLOCK), BLOCK)


def couple(off, at, chain, place, first, wide, unroll):
    height = SPACE - first
    table = jnp.concatenate(split(chain[first:SPACE, :]), axis=0)
    names, lanes = rows_iota(height, first), small(rows_iota(LANES, 0))

    def step(d, carry):
        where = place[pl.ds(d, 1), :]
        rows = jnp.dot(table, lane_one_hot(where, lanes), preferred_element_type=jnp.float32)
        hit = names == jnp.right_shift(where, 7)
        known = jnp.sum(jnp.where(hit, rows[:height] + rows[height:], 0.0), axis=0, keepdims=True)
        drop = jnp.sum(off[block_rows(d), at : at + REACH] * known, axis=1, keepdims=True)
        wide[block_rows(d), :] = jnp.broadcast_to(-drop, (BLOCK, LANES))
        return carry

    lax.fori_loop(0, BLOCKS, step, 0, unroll=unroll)


def fetch(pack, held, sems, cuts):
    copies = []
    for k, (first, last, to) in enumerate(cuts):
        copies.append(
            pltpu.make_async_copy(pack.at[:, first:last], held.at[:, to : to + last - first], sems.at[k])
        )
        copies[-1].start()
    return copies


def fetch_named(pack, named, sems, at):
    first = PLANE_NAMED_AT
    copies = [
        pltpu.make_async_copy(pack.at[:, first + k * LANES : first + (k + 1) * LANES], named.at[k], sems.at[at + k])
        for k in range(2)
    ]
    for copy in copies:
        copy.start()
    return copies


def chain_position(named, level, blocks):
    quarters = [
        named.at[a][pl.ds(2 * level + k, blocks, stride=BLOCK), :] for k in range(2) for a in range(2)
    ]
    return jnp.concatenate(quarters, axis=1).astype(jnp.int32) + (2 ** (level + 1) - 1) * LANES


def find_places(named, level, places):
    chain = chain_position(named, level, BLOCKS)
    if level == 0:
        block = lax.broadcasted_iota(jnp.int32, (BLOCKS, REACH), 0)
        places[...] = chain + jnp.where((chain < 3 * LANES) & (block < 16), 7 * LANES, 9 * LANES)
    else:
        places[...] = chain + 9 * LANES


def fetch_parts(parts, level, held, sems):
    first, last = LEVEL_AT[level]
    less = 0 if level < 3 else CUT
    copies, at = [], 0
    for k, part in enumerate(parts):
        count = part.shape[0]
        copies.append(
            pltpu.make_async_copy(part.at[:, first - less : last - less], held.at[pl.ds(at, count), :], sems.at[k])
        )
        copies[-1].start()
        at += count
    return copies


def path_solve(level, read, held, place, wide, total):
    diag_at, off_at = DIAG_AT[level] - LEVEL_AT[level][0], OFF_AT[level] - LEVEL_AT[level][0]
    for n in range(SPECIES):

        def write(at, value, n=n):
            wide[n, at : at + 64, :] = jnp.broadcast_to(value, (64, LANES))

        matvec(held, diag_at, 1, 2**level, functools.partial(read, n), write, OWN)
    names, lanes = small(rows_iota(PATH, 0)), small(rows_iota(LANES, 0))
    total[...] = jnp.zeros_like(total)

    def slot(d, carry):
        where = place[pl.ds(d, 1), :]
        hit = names == small(jnp.right_shift(where, 7))
        right = lane_one_hot(where, lanes)
        rows = block_rows(d)
        left = []
        for n in range(SPECIES):
            solved = jnp.concatenate([wide[n, rows, :]] * (REACH // LANES), axis=1)
            update = jnp.sum(held[rows, off_at : off_at + REACH] * solved, axis=0, keepdims=True)
            left += [pick(hit, part) for part in split(update)]
        total[...] += lax.dot_general(
            jnp.concatenate(left, axis=0), right, (((1,), (1,)), ((), ())), preferred_element_type=jnp.float32
        )
        return carry

    lax.fori_loop(0, SLOTS, slot, 0, unroll=4)


def path_update(level, before, total, path, ahead):
    count = 2 ** (level + 1)
    for n in range(SPECIES):
        at = 2 * n * PATH
        path[n * PATH : (n + 1) * PATH, :] = before[n * PATH : (n + 1) * PATH, :] - (
            total[at : at + PATH, :] + total[at + PATH : at + 2 * PATH, :]
        )
        if ahead is not None:
            ahead[n * count : (n + 1) * count, :] = path[n * PATH + count : n * PATH + 2 * count, :]


def path_first(*refs):
    parts = refs[: PARTS[0]]
    here, path, ahead, r0, places, held, named, turned, wide, total, sems = refs[PARTS[0] :]
    leaf, b = here[0], here[1]
    copies = fetch_parts(parts, 0, held, sems)
    path[...] = jnp.zeros((SPECIES * PATH, LANES), jnp.float32)
    lane = lax.broadcasted_iota(jnp.int32, (BLOCK, LANES), 1)
    row = lax.broadcasted_iota(jnp.int32, (BLOCK, LANES), 0)
    stands = []
    for core in (0, 1):
        for ahead_by in (0, 6, 2, 4):
            slot = jnp.bitwise_and(b + ahead_by, 7) ^ core
            stands.append(jnp.where(lane == row + slot * BLOCK, 1.0, 0.0).astype(jnp.bfloat16))
    order = jnp.concatenate(stands, axis=0)
    for copy in copies:
        copy.wait()
    flipped = jnp.transpose(held[:, RHS_AT : RHS_AT + 256])
    total_rows = None
    for _ in range(3):
        piece = flipped.astype(jnp.bfloat16)
        flipped = flipped - piece.astype(jnp.float32)
        rows = jnp.dot(piece, order, preferred_element_type=jnp.float32)
        total_rows = rows if total_rows is None else total_rows + rows
    turned[...] = total_rows
    for n in range(SPECIES):
        r0[n : n + 1, :] = turned[pl.ds(b * SPECIES + n, 1), :]
        for level in range(1, 6):
            at = n * PATH + 2**level + jnp.bitwise_and(leaf, 2**level - 1)
            path[pl.ds(at, 1), :] = turned[pl.ds(level * 32 + b * SPECIES + n, 1), :]
    for k in range(2):
        named[k] = held[:, NAMED_AT + k * LANES : NAMED_AT + (k + 1) * LANES]
    for level in range(5):
        places[level] = chain_position(named, level, SLOTS) + LANES
    path_solve(0, lambda n, c: r0[n : n + 1, :], held, places.at[0], wide, total)
    path_update(0, path, total, path, ahead)


def path_next(level, *refs):
    parts = refs[: PARTS[level]]
    places, summed, before, path, ahead, held, wide, total, sems = refs[PARTS[level] :]
    copies = fetch_parts(parts, level, held, sems)
    count = 2**level
    for copy in copies:
        copy.wait()
    path_solve(
        level, lambda n, c: summed[n * count + c : n * count + c + 1, :], held, places.at[level], wide, total
    )
    path_update(level, before, total, path, ahead)


def path_last(*refs):
    parts, (place, places, r0, r1, r2, r3, summed, before, keep, send, t2, t3, t4, path, *scratch) = (
        refs[: PARTS[4]], refs[PARTS[4] :]
    )
    path_next(4, *parts, places, summed, before, path, None, *scratch)
    x = place[0]
    even = 1.0 - (x & 1).astype(jnp.float32)
    for n in range(SPECIES):
        slot = n ^ x
        slot = slot ^ (slot >> 1)
        value = jnp.zeros((8, LANES), jnp.float32)
        row = lax.broadcasted_iota(jnp.int32, (8, LANES), 0)
        value = jnp.where(row == x, r0[n : n + 1, :], value)
        for k in range(2):
            value = jnp.where(row == 4 + 2 * (x >> 1) + k, r1[2 * n + k : 2 * n + k + 1, :] * even, value)
        for to, low in ((keep, 0), (send, 2)):

            @pl.when((slot >= low) & (slot < low + 2))
            def _(n=n, slot=slot, value=value, to=to, low=low):
                to[slot - low, 0:32, :] = path[n * PATH + 32 : (n + 1) * PATH, :]
                to[slot - low, 32:40, :] = value

    t2[...] = r2[pl.ds(x * 4, 4), :]
    t3[...] = r3[pl.ds(pl.multiple_of(x * 8, 8), 8), :]
    t4[...] = summed[pl.ds(pl.multiple_of(x * 16, 16), 16), :]


def high_cuts(level):
    columns = COUNT[level] * LANES
    return [
        (PLANE_DIAG_AT[level], PLANE_DIAG_AT[level] + columns, 0),
        (PLANE_OFF_AT[level], PLANE_OFF_AT[level] + REACH, columns),
    ]


def top(pack, summed, partial, held, wide, sems):
    pieces = 8
    size = ROWS // pieces

    def piece(k):
        rows = pl.ds(pl.multiple_of(k * size, size), size)
        columns = pl.ds(PLANE_DIAG_AT[5], COUNT[5] * LANES)
        return rows, pltpu.make_async_copy(pack.at[rows, columns], held.at[rows, :], sems.at[k])

    for k in range(pieces):
        piece(k)[1].start()
    partial[...] = jnp.zeros((COUNT[5], LANES), jnp.float32)

    @pl.loop(0, pieces)
    def _(k):
        rows, copy = piece(k)
        copy.wait()

        def write(at, value):
            wide[...] = jnp.broadcast_to(value, (size, LANES))

        matvec(held.at[rows, :], 0, 1, COUNT[5], lambda c: summed[c : c + 1, :], write, size)

        def write_row(c, value):
            partial[pl.ds(c, 1), :] = partial[pl.ds(c, 1), :] + value

        for c in range(COUNT[5]):
            term = held[rows, c * LANES : (c + 1) * LANES] * wide[...]
            write_row(c, jnp.sum(term, axis=0, keepdims=True))


def backward_high(level, pack, residual, *rest):
    above = rest[: 5 - level]
    partial, held, wide, chain, named, places, sems = rest[5 - level :]
    columns = COUNT[level] * LANES
    named_copies = fetch_named(pack, named, sems, 6)
    copies = fetch(pack, held, sems, high_cuts(level)[::-1])
    for k, value in enumerate(above):
        chain[FIRST[5 - k] : FIRST[5 - k] + COUNT[5 - k], :] = value[...]
    for copy in named_copies:
        copy.wait()
    find_places(named, level, places)
    copies[0].wait()
    couple(held, columns, chain, places, FIRST[level + 1], wide, BLOCKS)
    copies[1].wait()

    def write(at, value):
        wide[pl.ds(at, 64), :] = wide[pl.ds(at, 64), :] + value

    matvec(held, 0, 1, COUNT[level], lambda c: residual[c : c + 1, :], write)

    def write_row(c, value):
        partial[pl.ds(c, 1), :] = value

    matvec_transposed(held, 0, 1, COUNT[level], wide, write_row)


def backward_low(pack, r01, r2, s5, s4, s3, out, held, wide, chain, named, places, sems):
    named_copies = fetch_named(pack, named, sems, 6)
    cuts = []
    for level in (2, 1, 0):
        diag_at, off_at = PLANE_DIAG_AT[level], PLANE_OFF_AT[level]
        cuts.append((off_at, off_at + REACH, 896 + REACH * level))
        cuts.append((diag_at, diag_at + LANES * 2**level, LANES * (2**level - 1)))
    copies = fetch(pack, held, sems, cuts)
    for level, value in ((5, s5), (4, s4), (3, s3)):
        chain[FIRST[level] : FIRST[level] + COUNT[level], :] = value[...]
    chain[0:16, :] = jnp.zeros((16, LANES), jnp.float32)
    for copy in named_copies:
        copy.wait()
    for k, level in enumerate((2, 1, 0)):
        find_places(named, level, places)
        copies[2 * k].wait()
        couple(held, 896 + REACH * level, chain, places, 8, wide, BLOCKS // 2)

        def write(at, value):
            wide[pl.ds(at, 64), :] = wide[pl.ds(at, 64), :] + value

        def read(c, level=level):
            return r2[c : c + 1, :] if level == 2 else r01[4 * level + c : 4 * level + c + 1, :]

        copies[2 * k + 1].wait()
        matvec(held, LANES * (2**level - 1), 4 >> level, 1 << level, read, write)

        def write_row(c, value, first=FIRST[level]):
            chain[first + c : first + c + 1, :] = value

        matvec_transposed(held, LANES * (2**level - 1), 4 >> level, 1 << level, wide, write_row)
    out[...] = chain[0:16, :]


def call(body, outs, scratch, args, far=1, scalar=(), sems=8):
    vmem = pl.BlockSpec(memory_space=pltpu.VMEM)
    smem = pl.BlockSpec(memory_space=pltpu.SMEM)
    hbm = pl.BlockSpec(memory_space=pltpu.HBM)
    specs = [hbm if k < far else smem if k in scalar else vmem for k in range(len(args))]
    return pl.pallas_call(
        body,
        out_shape=outs,
        in_specs=specs,
        out_specs=jax.tree.map(lambda _: vmem, outs),
        scratch_shapes=scratch + [pltpu.SemaphoreType.DMA((sems,))],
        compiler_params=pltpu.CompilerParams(vmem_limit_bytes=(52 if far == 1 else 6) * MIB),
        cost_estimate=pl.CostEstimate(flops=2**29, bytes_accessed=2**20, transcendentals=0),
    )(*args)


def shape(*dims, kind=jnp.float32):
    return jax.ShapeDtypeStruct(dims, kind)


def moved(value, axis, to):
    size = lax.axis_size(axis)
    return lax.ppermute(value, axis, [(i, to(i)) for i in range(size)])


def near_x(i):
    return 3 - i


def far_z(i):
    return (i + 5) % 8 if i % 2 else (i + 3) % 8


def sum_leaf(value, first, last):
    steps = [("x", lambda i: i ^ 1), ("x", near_x), ("z", lambda i: i ^ 1)]
    if last < 5:
        steps.append(("z", lambda i: i ^ 2))
    else:
        steps.append(("z", lambda i: (i + 1) % 8 if i % 2 else (i + 7) % 8))
        steps.append(("z", far_z))
    for axis, to in steps[first:last]:
        value = value + moved(value, axis, to)
    return value


def local(rhs, diag_inverse, off_diagonal, rows_index):
    f32 = jnp.float32
    x, z = lax.axis_index("x"), lax.axis_index("z")
    leaf = z * 4 + x
    hbm, vmem = pl.BlockSpec(memory_space=pltpu.HBM), pl.BlockSpec(memory_space=pltpu.VMEM)
    pack, first, second = pl.pallas_call(
        pack_all,
        out_shape=(shape(BLOCK, WHOLE), shape(BLOCK, CUT), shape(BLOCK, GROUP - CUT)),
        in_specs=[vmem, vmem, hbm, hbm],
        out_specs=(vmem,) * 3,
        scratch_shapes=[pltpu.SemaphoreType.DMA((16,))],
        compiler_params=pltpu.CompilerParams(vmem_limit_bytes=6 * MIB),
    )(jnp.transpose(rhs, (0, 2, 1)), rows_index, diag_inverse, off_diagonal)
    pack = lax.all_gather(pack, PLANE, axis=0, tiled=True)

    def other_core(parts):
        return parts + tuple(moved(part, "blk", lambda i: i ^ 1) for part in parts)

    def this_core(own):
        return (own,) + tuple(moved(own, "blk", lambda i, hop=hop: (i + hop) % SLOTS) for hop in (2, 6, 4))

    first = other_core(this_core(first))
    second = this_core(lax.optimization_barrier((second, first[-1]))[0])

    def path_scratch(level, *more):
        return [
            pltpu.VMEM((OWN, LEVEL_AT[level][1] - LEVEL_AT[level][0]), f32),
            *more,
            pltpu.VMEM((SPECIES, OWN, LANES), f32),
            pltpu.VMEM((SPECIES * 2 * PATH, LANES), f32),
        ]

    here = jnp.stack([leaf, lax.axis_index("blk")]).astype(jnp.int32)
    path, ahead, r0, places = call(
        path_first,
        (
            shape(SPECIES * PATH, LANES), shape(SPECIES * 2, LANES), shape(SPECIES, LANES),
            shape(5, SLOTS, REACH, kind=jnp.int32),
        ),
        path_scratch(0, pltpu.VMEM((2, OWN, LANES), f32), pltpu.VMEM((256, LANES), f32)),
        (*first, here),
        far=PARTS[0],
        scalar=(PARTS[0],),
        sems=PARTS[0],
    )
    waiting = [r0, sum_leaf(ahead, 0, 1)]
    for level in (1, 2, 3):
        path, ahead = call(
            functools.partial(path_next, level),
            (shape(SPECIES * PATH, LANES), shape(SPECIES * 2 ** (level + 1), LANES)),
            path_scratch(level),
            (*(first if level < 3 else second), places, waiting[level], path),
            far=PARTS[level],
            sems=PARTS[level],
        )
        if level == 2:
            second = other_core(lax.optimization_barrier((*second, ahead))[:4])
        waiting.append(sum_leaf(ahead, 0, level + 1))
    keep, send, r2, r3, r4 = call(
        path_last,
        (shape(2, 40, LANES), shape(2, 40, LANES), shape(4, LANES), shape(8, LANES), shape(16, LANES)),
        [pltpu.VMEM((SPECIES * PATH, LANES), f32)] + path_scratch(4),
        (*second, x.astype(jnp.int32).reshape(1), places, *waiting, path),
        far=PARTS[4],
        scalar=(PARTS[4],),
        sems=PARTS[4],
    )
    keep = keep + moved(send, "x", near_x)
    turned = keep[0] + moved(keep[1], "x", lambda i: i ^ 1)
    r5 = sum_leaf(turned[0:32], 2, 5)

    wide, chain = pltpu.VMEM((ROWS, LANES), f32), pltpu.VMEM((SPACE, LANES), f32)
    named, places = pltpu.VMEM((2, ROWS, LANES), f32), pltpu.VMEM((BLOCKS, REACH), jnp.int32)
    partial = call(top, shape(32, LANES), [pltpu.VMEM((ROWS, 32 * LANES), f32), pltpu.VMEM((ROWS // 8, LANES), f32)], (pack, r5))
    known = [sum_leaf(partial, 2, 5)]
    for level, from_rows in ((4, r4), (3, r3)):
        count = COUNT[level]
        partial = call(
            functools.partial(backward_high, level),
            shape(count, LANES),
            [pltpu.VMEM((ROWS, count * LANES + REACH), f32), wide, chain, named, places],
            (pack, from_rows, *known),
        )
        known.append(sum_leaf(partial, 2, level))
    last = call(
        backward_low,
        shape(16, LANES),
        [pltpu.VMEM((ROWS, 896 + 3 * REACH), f32), wide, chain, named, places],
        (pack, turned[32:40], r2, *known),
    )
    pieces = [last[0:4], last[8:12], last[12:16]]
    for level in (3, 4, 5):
        place = jnp.remainder(z, 2 ** (level - 2)) * 4
        pieces.append(lax.dynamic_slice_in_dim(known[5 - level], place, 4, 0))
    out = jnp.stack(pieces).reshape(6, BLOCKS, BLOCK)
    out = lax.all_to_all(jnp.transpose(out, (1, 0, 2)), PLANE, 0, 0)
    return jnp.transpose(out.reshape(SPECIES, SLOTS, 6, BLOCK), (2, 1, 0, 3)).reshape(6, BLOCKS, BLOCK)


def solution(mesh):
    cut = Mesh(mesh.devices.reshape(8, 4, 8), ("z", "x", "blk"))
    rows = ("z", "x", "blk")
    placed = (P(None, None, rows), P(rows, None), P(None, rows, None), P(None, rows, None))
    return jax.shard_map(
        local, mesh=cut, in_specs=placed, out_specs=P(None, None, rows), check_vma=False
    )
```

```python
import functools

import jax
import jax.numpy as jnp
from jax import lax
from jax.experimental import pallas as pl
from jax.experimental.pallas import tpu as pltpu
from jax.sharding import Mesh
from jax.sharding import PartitionSpec as P

PLANE = ("x", "blk")
LANES = 128
BLOCK = 16
BLOCKS = 32
ROWS = BLOCK * BLOCKS
REACH = 512
SLOTS = 8
OWN = SLOTS * BLOCK
SPECIES = 4
FIRST = (0, 8, 12, 16, 24, 40)
COUNT = (4, 4, 4, 8, 16, 32)
SPACE = 72
PATH = 64
PARTS = (8, 8, 8, 8, 8)
RHS_AT = 0
NAMED_AT = 256
DIAG_AT = (512, 1152, 1920, 2944, 4480)
OFF_AT = (640, 1408, 2432, 3968, 6528)
CUT = 2944
GROUP = 7040
LEVEL_AT = ((0, 1152), (1152, 1920), (1920, 2944), (2944, 4480), (4480, 7040))
PLANE_DIAG_AT = (0, 128, 384, 896, 1920, 3968)
PLANE_OFF_AT = (8064, 8576, 9088, 9600, 10112)
PLANE_NAMED_AT = 10624
WHOLE = 10880
MIB = 1024 * 1024


def store_named(rows_index, to, at):
    for level in range(5):
        for k in range(2):
            named = rows_index[level, :, k * 256 : (k + 1) * 256].astype(jnp.float32)
            to[2 * level + k : 2 * level + k + 1, at : at + 256] = named
    to[10:16, at : at + 256] = jnp.zeros((6, 256), jnp.float32)


def start_all(moves, sems):
    copies = [pltpu.make_async_copy(source, target, sems.at[k]) for k, (source, target) in enumerate(moves)]
    for copy in copies:
        copy.start()
    return copies


def pack_all(rhs, rows_index, diag_inverse, off_diagonal, pack, first, second, sems):
    moves = []
    for level in range(5):
        part, less = (first, 0) if level < 3 else (second, CUT)
        columns = 2**level * LANES
        diag_at, off_at = DIAG_AT[level] - less, OFF_AT[level] - less
        diag = diag_inverse.at[:, columns - LANES : 2 * columns - LANES]
        moves.append((diag, part.at[:, diag_at : diag_at + columns]))
        moves.append((off_diagonal.at[level], part.at[:, off_at : off_at + REACH]))
    moves.append((diag_inverse, pack.at[:, 0:8064]))
    for level in range(5):
        at = PLANE_OFF_AT[level]
        moves.append((off_diagonal.at[level], pack.at[:, at : at + REACH]))
    copies = start_all(moves, sems)
    given = [rhs[level] for level in range(6)] + [jnp.zeros((BLOCK, 64), jnp.float32)]
    first[:, RHS_AT : RHS_AT + 256] = jnp.concatenate(given, axis=1)
    store_named(rows_index, first, NAMED_AT)
    store_named(rows_index, pack, PLANE_NAMED_AT)
    for copy in copies:
        copy.wait()


def matvec(diag, at, groups, chunks, read_row, write, rows=ROWS):
    size = rows // groups

    def step(k, start):
        total = None
        for c in range(chunks):
            term = diag[pl.ds(start, 64), at + c * LANES : at + (c + 1) * LANES] * read_row(k * chunks + c)
            total = term if total is None else total + term
        write(start, jnp.sum(total, axis=1, keepdims=True))

    for k in range(groups):
        for start in range(k * size, (k + 1) * size, 64):
            step(k, start)


def matvec_transposed(diag, at, groups, chunks, wide, write, rows=ROWS):
    size = rows // groups

    def step(k, c):
        total = None
        for start in range(k * size, (k + 1) * size, 64):
            columns = pl.ds(at + c * LANES, LANES) if isinstance(c, int) else pl.ds(pl.multiple_of(at + c * LANES, LANES), LANES)
            term = diag[start : start + 64, columns] * wide[start : start + 64, :]
            total = term if total is None else total + term
        write(k * chunks + c, jnp.sum(total, axis=0, keepdims=True))

    for k in range(groups):
        for c in range(chunks):
            step(k, c)


def split(value):
    coarse = value.astype(jnp.bfloat16)
    return coarse, (value - coarse.astype(jnp.float32)).astype(jnp.bfloat16)


def rows_iota(rows, first):
    return lax.broadcasted_iota(jnp.int32, (rows, REACH), 0) + first


def small(whole):
    return whole.astype(jnp.float32).astype(jnp.bfloat16)


def pick(hit, value):
    return jnp.where(hit, value, jnp.zeros((), jnp.bfloat16))


def lane_one_hot(where, lanes):
    return pick(lanes == small(jnp.bitwise_and(where, 127)), jnp.ones((), jnp.bfloat16))


def block_rows(d):
    return pl.ds(pl.multiple_of(d * BLOCK, BLOCK), BLOCK)


def couple(off, at, chain, place, first, wide, unroll):
    height = SPACE - first
    table = jnp.concatenate(split(chain[first:SPACE, :]), axis=0)
    names, lanes = rows_iota(height, first), small(rows_iota(LANES, 0))

    def step(d, carry):
        where = place[pl.ds(d, 1), :]
        rows = jnp.dot(table, lane_one_hot(where, lanes), preferred_element_type=jnp.float32)
        hit = names == jnp.right_shift(where, 7)
        known = jnp.sum(jnp.where(hit, rows[:height] + rows[height:], 0.0), axis=0, keepdims=True)
        drop = jnp.sum(off[block_rows(d), at : at + REACH] * known, axis=1, keepdims=True)
        wide[block_rows(d), :] = jnp.broadcast_to(-drop, (BLOCK, LANES))
        return carry

    lax.fori_loop(0, BLOCKS, step, 0, unroll=unroll)


def fetch(pack, held, sems, cuts):
    copies = []
    for k, (first, last, to) in enumerate(cuts):
        copies.append(
            pltpu.make_async_copy(pack.at[:, first:last], held.at[:, to : to + last - first], sems.at[k])
        )
        copies[-1].start()
    return copies


def fetch_named(pack, named, sems, at):
    first = PLANE_NAMED_AT
    copies = [
        pltpu.make_async_copy(pack.at[:, first + k * LANES : first + (k + 1) * LANES], named.at[k], sems.at[at + k])
        for k in range(2)
    ]
    for copy in copies:
        copy.start()
    return copies


def chain_position(named, level, blocks):
    quarters = [
        named.at[a][pl.ds(2 * level + k, blocks, stride=BLOCK), :] for k in range(2) for a in range(2)
    ]
    return jnp.concatenate(quarters, axis=1).astype(jnp.int32) + (2 ** (level + 1) - 1) * LANES


def find_places(named, level, places):
    chain = chain_position(named, level, BLOCKS)
    if level == 0:
        block = lax.broadcasted_iota(jnp.int32, (BLOCKS, REACH), 0)
        places[...] = chain + jnp.where((chain < 3 * LANES) & (block < 16), 7 * LANES, 9 * LANES)
    else:
        places[...] = chain + 9 * LANES


def fetch_parts(parts, level, held, sems):
    first, last = LEVEL_AT[level]
    less = 0 if level < 3 else CUT
    copies, at = [], 0
    for k, part in enumerate(parts):
        count = part.shape[0]
        copies.append(
            pltpu.make_async_copy(part.at[:, first - less : last - less], held.at[pl.ds(at, count), :], sems.at[k])
        )
        copies[-1].start()
        at += count
    return copies


def path_solve(level, read, held, place, wide, total):
    diag_at, off_at = DIAG_AT[level] - LEVEL_AT[level][0], OFF_AT[level] - LEVEL_AT[level][0]
    for n in range(SPECIES):

        def write(at, value, n=n):
            wide[n, at : at + 64, :] = jnp.broadcast_to(value, (64, LANES))

        matvec(held, diag_at, 1, 2**level, functools.partial(read, n), write, OWN)
    names, lanes = small(rows_iota(PATH, 0)), small(rows_iota(LANES, 0))
    total[...] = jnp.zeros_like(total)

    def slot(d, carry):
        where = place[pl.ds(d, 1), :]
        hit = names == small(jnp.right_shift(where, 7))
        right = lane_one_hot(where, lanes)
        rows = block_rows(d)
        left = []
        for n in range(SPECIES):
            solved = jnp.concatenate([wide[n, rows, :]] * (REACH // LANES), axis=1)
            update = jnp.sum(held[rows, off_at : off_at + REACH] * solved, axis=0, keepdims=True)
            left += [pick(hit, part) for part in split(update)]
        total[...] += lax.dot_general(
            jnp.concatenate(left, axis=0), right, (((1,), (1,)), ((), ())), preferred_element_type=jnp.float32
        )
        return carry

    lax.fori_loop(0, SLOTS, slot, 0, unroll=4)


def path_update(level, before, total, path, ahead):
    count = 2 ** (level + 1)
    for n in range(SPECIES):
        at = 2 * n * PATH
        path[n * PATH : (n + 1) * PATH, :] = before[n * PATH : (n + 1) * PATH, :] - (
            total[at : at + PATH, :] + total[at + PATH : at + 2 * PATH, :]
        )
        if ahead is not None:
            ahead[n * count : (n + 1) * count, :] = path[n * PATH + count : n * PATH + 2 * count, :]


def path_first(*refs):
    parts = refs[: PARTS[0]]
    here, path, ahead, r0, places, held, named, turned, wide, total, sems = refs[PARTS[0] :]
    leaf, b = here[0], here[1]
    copies = fetch_parts(parts, 0, held, sems)
    path[...] = jnp.zeros((SPECIES * PATH, LANES), jnp.float32)
    lane = lax.broadcasted_iota(jnp.int32, (BLOCK, LANES), 1)
    row = lax.broadcasted_iota(jnp.int32, (BLOCK, LANES), 0)
    stands = []
    for core in (0, 1):
        for ahead_by in (0, 6, 2, 4):
            slot = jnp.bitwise_and(b + ahead_by, 7) ^ core
            stands.append(jnp.where(lane == row + slot * BLOCK, 1.0, 0.0).astype(jnp.bfloat16))
    order = jnp.concatenate(stands, axis=0)
    for copy in copies:
        copy.wait()
    flipped = jnp.transpose(held[:, RHS_AT : RHS_AT + 256])
    total_rows = None
    for _ in range(3):
        piece = flipped.astype(jnp.bfloat16)
        flipped = flipped - piece.astype(jnp.float32)
        rows = jnp.dot(piece, order, preferred_element_type=jnp.float32)
        total_rows = rows if total_rows is None else total_rows + rows
    turned[...] = total_rows
    for n in range(SPECIES):
        r0[n : n + 1, :] = turned[pl.ds(b * SPECIES + n, 1), :]
        for level in range(1, 6):
            at = n * PATH + 2**level + jnp.bitwise_and(leaf, 2**level - 1)
            path[pl.ds(at, 1), :] = turned[pl.ds(level * 32 + b * SPECIES + n, 1), :]
    for k in range(2):
        named[k] = held[:, NAMED_AT + k * LANES : NAMED_AT + (k + 1) * LANES]
    for level in range(5):
        places[level] = chain_position(named, level, SLOTS) + LANES
    path_solve(0, lambda n, c: r0[n : n + 1, :], held, places.at[0], wide, total)
    path_update(0, path, total, path, ahead)


def path_next(level, *refs):
    parts = refs[: PARTS[level]]
    places, summed, before, path, ahead, held, wide, total, sems = refs[PARTS[level] :]
    copies = fetch_parts(parts, level, held, sems)
    count = 2**level
    for copy in copies:
        copy.wait()
    path_solve(
        level, lambda n, c: summed[n * count + c : n * count + c + 1, :], held, places.at[level], wide, total
    )
    path_update(level, before, total, path, ahead)


def path_last(*refs):
    parts, (place, places, r0, r1, r2, r3, summed, before, keep, send, t2, t3, t4, path, *scratch) = (
        refs[: PARTS[4]], refs[PARTS[4] :]
    )
    path_next(4, *parts, places, summed, before, path, None, *scratch)
    x = place[0]
    even = 1.0 - (x & 1).astype(jnp.float32)
    for n in range(SPECIES):
        slot = n ^ x
        slot = slot ^ (slot >> 1)
        value = jnp.zeros((8, LANES), jnp.float32)
        row = lax.broadcasted_iota(jnp.int32, (8, LANES), 0)
        value = jnp.where(row == x, r0[n : n + 1, :], value)
        for k in range(2):
            value = jnp.where(row == 4 + 2 * (x >> 1) + k, r1[2 * n + k : 2 * n + k + 1, :] * even, value)
        for to, low in ((keep, 0), (send, 2)):

            @pl.when((slot >= low) & (slot < low + 2))
            def _(n=n, slot=slot, value=value, to=to, low=low):
                to[slot - low, 0:32, :] = path[n * PATH + 32 : (n + 1) * PATH, :]
                to[slot - low, 32:40, :] = value

    t2[...] = r2[pl.ds(x * 4, 4), :]
    t3[...] = r3[pl.ds(pl.multiple_of(x * 8, 8), 8), :]
    t4[...] = summed[pl.ds(pl.multiple_of(x * 16, 16), 16), :]


def high_cuts(level):
    columns = COUNT[level] * LANES
    return [
        (PLANE_DIAG_AT[level], PLANE_DIAG_AT[level] + columns, 0),
        (PLANE_OFF_AT[level], PLANE_OFF_AT[level] + REACH, columns),
    ]


def top(pack, summed, partial, held, wide, sems):
    pieces = 8
    size = ROWS // pieces

    def piece(k):
        rows = pl.ds(pl.multiple_of(k * size, size), size)
        columns = pl.ds(PLANE_DIAG_AT[5], COUNT[5] * LANES)
        return rows, pltpu.make_async_copy(pack.at[rows, columns], held.at[rows, :], sems.at[k])

    for k in range(pieces):
        piece(k)[1].start()
    partial[...] = jnp.zeros((COUNT[5], LANES), jnp.float32)

    @pl.loop(0, pieces)
    def _(k):
        rows, copy = piece(k)
        copy.wait()

        def write(at, value):
            wide[...] = jnp.broadcast_to(value, (size, LANES))

        matvec(held.at[rows, :], 0, 1, COUNT[5], lambda c: summed[c : c + 1, :], write, size)

        def write_row(c, value):
            partial[pl.ds(c, 1), :] = partial[pl.ds(c, 1), :] + value

        for c in range(COUNT[5]):
            term = held[rows, c * LANES : (c + 1) * LANES] * wide[...]
            write_row(c, jnp.sum(term, axis=0, keepdims=True))


def backward_high(level, pack, residual, *rest):
    above = rest[: 5 - level]
    partial, held, wide, chain, named, places, sems = rest[5 - level :]
    columns = COUNT[level] * LANES
    named_copies = fetch_named(pack, named, sems, 6)
    copies = fetch(pack, held, sems, high_cuts(level)[::-1])
    for k, value in enumerate(above):
        chain[FIRST[5 - k] : FIRST[5 - k] + COUNT[5 - k], :] = value[...]
    for copy in named_copies:
        copy.wait()
    find_places(named, level, places)
    copies[0].wait()
    couple(held, columns, chain, places, FIRST[level + 1], wide, BLOCKS)
    copies[1].wait()

    def write(at, value):
        wide[pl.ds(at, 64), :] = wide[pl.ds(at, 64), :] + value

    matvec(held, 0, 1, COUNT[level], lambda c: residual[c : c + 1, :], write)

    def write_row(c, value):
        partial[pl.ds(c, 1), :] = value

    matvec_transposed(held, 0, 1, COUNT[level], wide, write_row)


def backward_low(pack, r01, r2, s5, s4, s3, out, held, wide, chain, named, places, sems):
    named_copies = fetch_named(pack, named, sems, 6)
    cuts = []
    for level in (2, 1, 0):
        diag_at, off_at = PLANE_DIAG_AT[level], PLANE_OFF_AT[level]
        cuts.append((off_at, off_at + REACH, 896 + REACH * level))
        cuts.append((diag_at, diag_at + LANES * 2**level, LANES * (2**level - 1)))
    copies = fetch(pack, held, sems, cuts)
    for level, value in ((5, s5), (4, s4), (3, s3)):
        chain[FIRST[level] : FIRST[level] + COUNT[level], :] = value[...]
    chain[0:16, :] = jnp.zeros((16, LANES), jnp.float32)
    for copy in named_copies:
        copy.wait()
    for k, level in enumerate((2, 1, 0)):
        find_places(named, level, places)
        copies[2 * k].wait()
        couple(held, 896 + REACH * level, chain, places, 8, wide, BLOCKS)

        def write(at, value):
            wide[pl.ds(at, 64), :] = wide[pl.ds(at, 64), :] + value

        def read(c, level=level):
            return r2[c : c + 1, :] if level == 2 else r01[4 * level + c : 4 * level + c + 1, :]

        copies[2 * k + 1].wait()
        matvec(held, LANES * (2**level - 1), 4 >> level, 1 << level, read, write)

        def write_row(c, value, first=FIRST[level]):
            chain[first + c : first + c + 1, :] = value

        matvec_transposed(held, LANES * (2**level - 1), 4 >> level, 1 << level, wide, write_row)
    out[...] = chain[0:16, :]


def call(body, outs, scratch, args, far=1, scalar=(), sems=8):
    vmem = pl.BlockSpec(memory_space=pltpu.VMEM)
    smem = pl.BlockSpec(memory_space=pltpu.SMEM)
    hbm = pl.BlockSpec(memory_space=pltpu.HBM)
    specs = [hbm if k < far else smem if k in scalar else vmem for k in range(len(args))]
    return pl.pallas_call(
        body,
        out_shape=outs,
        in_specs=specs,
        out_specs=jax.tree.map(lambda _: vmem, outs),
        scratch_shapes=scratch + [pltpu.SemaphoreType.DMA((sems,))],
        compiler_params=pltpu.CompilerParams(vmem_limit_bytes=(52 if far == 1 else 6) * MIB),
        cost_estimate=pl.CostEstimate(flops=2**29, bytes_accessed=2**20, transcendentals=0),
    )(*args)


def shape(*dims, kind=jnp.float32):
    return jax.ShapeDtypeStruct(dims, kind)


def moved(value, axis, to):
    size = lax.axis_size(axis)
    return lax.ppermute(value, axis, [(i, to(i)) for i in range(size)])


def near_x(i):
    return 3 - i


def far_z(i):
    return (i + 5) % 8 if i % 2 else (i + 3) % 8


def sum_leaf(value, first, last):
    steps = [("x", lambda i: i ^ 1), ("x", near_x), ("z", lambda i: i ^ 1)]
    if last < 5:
        steps.append(("z", lambda i: i ^ 2))
    else:
        steps.append(("z", lambda i: (i + 1) % 8 if i % 2 else (i + 7) % 8))
        steps.append(("z", far_z))
    for axis, to in steps[first:last]:
        value = value + moved(value, axis, to)
    return value


def local(rhs, diag_inverse, off_diagonal, rows_index):
    f32 = jnp.float32
    x, z = lax.axis_index("x"), lax.axis_index("z")
    leaf = z * 4 + x
    hbm, vmem = pl.BlockSpec(memory_space=pltpu.HBM), pl.BlockSpec(memory_space=pltpu.VMEM)
    pack, first, second = pl.pallas_call(
        pack_all,
        out_shape=(shape(BLOCK, WHOLE), shape(BLOCK, CUT), shape(BLOCK, GROUP - CUT)),
        in_specs=[vmem, vmem, hbm, hbm],
        out_specs=(vmem,) * 3,
        scratch_shapes=[pltpu.SemaphoreType.DMA((16,))],
        compiler_params=pltpu.CompilerParams(vmem_limit_bytes=56 * MIB),
    )(jnp.transpose(rhs, (0, 2, 1)), rows_index, diag_inverse, off_diagonal)
    pack = lax.all_gather(pack, PLANE, axis=0, tiled=True)

    def other_core(parts):
        return parts + tuple(moved(part, "blk", lambda i: i ^ 1) for part in parts)

    def this_core(own):
        return (own,) + tuple(moved(own, "blk", lambda i, hop=hop: (i + hop) % SLOTS) for hop in (2, 6, 4))

    first = other_core(this_core(first))
    second = this_core(lax.optimization_barrier((second, first[-1]))[0])

    def path_scratch(level, *more):
        return [
            pltpu.VMEM((OWN, LEVEL_AT[level][1] - LEVEL_AT[level][0]), f32),
            *more,
            pltpu.VMEM((SPECIES, OWN, LANES), f32),
            pltpu.VMEM((SPECIES * 2 * PATH, LANES), f32),
        ]

    here = jnp.stack([leaf, lax.axis_index("blk")]).astype(jnp.int32)
    path, ahead, r0, places = call(
        path_first,
        (
            shape(SPECIES * PATH, LANES), shape(SPECIES * 2, LANES), shape(SPECIES, LANES),
            shape(5, SLOTS, REACH, kind=jnp.int32),
        ),
        path_scratch(0, pltpu.VMEM((2, OWN, LANES), f32), pltpu.VMEM((256, LANES), f32)),
        (*first, here),
        far=PARTS[0],
        scalar=(PARTS[0],),
        sems=PARTS[0],
    )
    waiting = [r0, sum_leaf(ahead, 0, 1)]
    for level in (1, 2, 3):
        path, ahead = call(
            functools.partial(path_next, level),
            (shape(SPECIES * PATH, LANES), shape(SPECIES * 2 ** (level + 1), LANES)),
            path_scratch(level),
            (*(first if level < 3 else second), places, waiting[level], path),
            far=PARTS[level],
            sems=PARTS[level],
        )
        if level == 2:
            second = other_core(lax.optimization_barrier((*second, ahead))[:4])
        waiting.append(sum_leaf(ahead, 0, level + 1))
    keep, send, r2, r3, r4 = call(
        path_last,
        (shape(2, 40, LANES), shape(2, 40, LANES), shape(4, LANES), shape(8, LANES), shape(16, LANES)),
        [pltpu.VMEM((SPECIES * PATH, LANES), f32)] + path_scratch(4),
        (*second, x.astype(jnp.int32).reshape(1), places, *waiting, path),
        far=PARTS[4],
        scalar=(PARTS[4],),
        sems=PARTS[4],
    )
    keep = keep + moved(send, "x", near_x)
    turned = keep[0] + moved(keep[1], "x", lambda i: i ^ 1)
    r5 = sum_leaf(turned[0:32], 2, 5)

    wide, chain = pltpu.VMEM((ROWS, LANES), f32), pltpu.VMEM((SPACE, LANES), f32)
    named, places = pltpu.VMEM((2, ROWS, LANES), f32), pltpu.VMEM((BLOCKS, REACH), jnp.int32)
    partial = call(top, shape(32, LANES), [pltpu.VMEM((ROWS, 32 * LANES), f32), pltpu.VMEM((ROWS // 8, LANES), f32)], (pack, r5))
    known = [sum_leaf(partial, 2, 5)]
    for level, from_rows in ((4, r4), (3, r3)):
        count = COUNT[level]
        partial = call(
            functools.partial(backward_high, level),
            shape(count, LANES),
            [pltpu.VMEM((ROWS, count * LANES + REACH), f32), wide, chain, named, places],
            (pack, from_rows, *known),
        )
        known.append(sum_leaf(partial, 2, level))
    last = call(
        backward_low,
        shape(16, LANES),
        [pltpu.VMEM((ROWS, 896 + 3 * REACH), f32), wide, chain, named, places],
        (pack, turned[32:40], r2, *known),
    )
    pieces = [last[0:4], last[8:12], last[12:16]]
    for level in (3, 4, 5):
        place = jnp.remainder(z, 2 ** (level - 2)) * 4
        pieces.append(lax.dynamic_slice_in_dim(known[5 - level], place, 4, 0))
    out = jnp.stack(pieces).reshape(6, BLOCKS, BLOCK)
    out = lax.all_to_all(jnp.transpose(out, (1, 0, 2)), PLANE, 0, 0)
    return jnp.transpose(out.reshape(SPECIES, SLOTS, 6, BLOCK), (2, 1, 0, 3)).reshape(6, BLOCKS, BLOCK)


def solution(mesh):
    cut = Mesh(mesh.devices.reshape(8, 4, 8), ("z", "x", "blk"))
    rows = ("z", "x", "blk")
    placed = (P(None, None, rows), P(rows, None), P(None, rows, None), P(None, rows, None))
    return jax.shard_map(
        local, mesh=cut, in_specs=placed, out_specs=P(None, None, rows), check_vma=False
    )
```

```python
import functools

import jax
import jax.numpy as jnp
from jax import lax
from jax.experimental import pallas as pl
from jax.experimental.pallas import tpu as pltpu
from jax.sharding import Mesh
from jax.sharding import PartitionSpec as P

PLANE = ("x", "blk")
LANES = 128
BLOCK = 16
BLOCKS = 32
ROWS = BLOCK * BLOCKS
REACH = 512
SLOTS = 8
OWN = SLOTS * BLOCK
SPECIES = 4
FIRST = (0, 8, 12, 16, 24, 40)
COUNT = (4, 4, 4, 8, 16, 32)
SPACE = 72
PATH = 64
PARTS = (8, 8, 8, 8, 8)
RHS_AT = 0
NAMED_AT = 256
DIAG_AT = (512, 1152, 1920, 2944, 4480)
OFF_AT = (640, 1408, 2432, 3968, 6528)
CUT = 2944
GROUP = 7040
LEVEL_AT = ((0, 1152), (1152, 1920), (1920, 2944), (2944, 4480), (4480, 7040))
PLANE_DIAG_AT = (0, 128, 384, 896, 1920, 3968)
PLANE_OFF_AT = (8064, 8576, 9088, 9600, 10112)
PLANE_NAMED_AT = 10624
WHOLE = 10880
MIB = 1024 * 1024


def store_named(rows_index, to, at):
    for level in range(5):
        for k in range(2):
            named = rows_index[level, :, k * 256 : (k + 1) * 256].astype(jnp.float32)
            to[2 * level + k : 2 * level + k + 1, at : at + 256] = named
    to[10:16, at : at + 256] = jnp.zeros((6, 256), jnp.float32)


def start_all(moves, sems):
    copies = [pltpu.make_async_copy(source, target, sems.at[k]) for k, (source, target) in enumerate(moves)]
    for copy in copies:
        copy.start()
    return copies


def pack_all(rhs, rows_index, diag_inverse, off_diagonal, pack, first, second, sems):
    moves = []
    for level in range(5):
        part, less = (first, 0) if level < 3 else (second, CUT)
        columns = 2**level * LANES
        diag_at, off_at = DIAG_AT[level] - less, OFF_AT[level] - less
        diag = diag_inverse.at[:, columns - LANES : 2 * columns - LANES]
        moves.append((diag, part.at[:, diag_at : diag_at + columns]))
        moves.append((off_diagonal.at[level], part.at[:, off_at : off_at + REACH]))
    moves.append((diag_inverse, pack.at[:, 0:8064]))
    for level in range(5):
        at = PLANE_OFF_AT[level]
        moves.append((off_diagonal.at[level], pack.at[:, at : at + REACH]))
    copies = start_all(moves, sems)
    given = [rhs[level] for level in range(6)] + [jnp.zeros((BLOCK, 64), jnp.float32)]
    first[:, RHS_AT : RHS_AT + 256] = jnp.concatenate(given, axis=1)
    store_named(rows_index, first, NAMED_AT)
    store_named(rows_index, pack, PLANE_NAMED_AT)
    for copy in copies:
        copy.wait()


def matvec(diag, at, groups, chunks, read_row, write, rows=ROWS):
    size = rows // groups

    def step(k, start):
        total = None
        for c in range(chunks):
            term = diag[pl.ds(start, 64), at + c * LANES : at + (c + 1) * LANES] * read_row(k * chunks + c)
            total = term if total is None else total + term
        write(start, jnp.sum(total, axis=1, keepdims=True))

    for k in range(groups):
        for start in range(k * size, (k + 1) * size, 64):
            step(k, start)


def matvec_transposed(diag, at, groups, chunks, wide, write, rows=ROWS):
    size = rows // groups

    def step(k, c):
        total = None
        for start in range(k * size, (k + 1) * size, 64):
            columns = pl.ds(at + c * LANES, LANES) if isinstance(c, int) else pl.ds(pl.multiple_of(at + c * LANES, LANES), LANES)
            term = diag[start : start + 64, columns] * wide[start : start + 64, :]
            total = term if total is None else total + term
        write(k * chunks + c, jnp.sum(total, axis=0, keepdims=True))

    for k in range(groups):
        for c in range(chunks):
            step(k, c)


def split(value):
    coarse = value.astype(jnp.bfloat16)
    return coarse, (value - coarse.astype(jnp.float32)).astype(jnp.bfloat16)


def rows_iota(rows, first):
    return lax.broadcasted_iota(jnp.int32, (rows, REACH), 0) + first


def small(whole):
    return whole.astype(jnp.float32).astype(jnp.bfloat16)


def pick(hit, value):
    return jnp.where(hit, value, jnp.zeros((), jnp.bfloat16))


def lane_one_hot(where, lanes):
    return pick(lanes == small(jnp.bitwise_and(where, 127)), jnp.ones((), jnp.bfloat16))


def block_rows(d):
    return pl.ds(pl.multiple_of(d * BLOCK, BLOCK), BLOCK)


def couple(off, at, chain, place, first, wide, unroll):
    height = SPACE - first
    table = jnp.concatenate(split(chain[first:SPACE, :]), axis=0)
    names, lanes = rows_iota(height, first), small(rows_iota(LANES, 0))

    def step(d, carry):
        where = place[pl.ds(d, 1), :]
        rows = jnp.dot(table, lane_one_hot(where, lanes), preferred_element_type=jnp.float32)
        hit = names == jnp.right_shift(where, 7)
        known = jnp.sum(jnp.where(hit, rows[:height] + rows[height:], 0.0), axis=0, keepdims=True)
        drop = jnp.sum(off[block_rows(d), at : at + REACH] * known, axis=1, keepdims=True)
        wide[block_rows(d), :] = jnp.broadcast_to(-drop, (BLOCK, LANES))
        return carry

    lax.fori_loop(0, BLOCKS, step, 0, unroll=unroll)


def fetch(pack, held, sems, cuts):
    copies = []
    for k, (first, last, to) in enumerate(cuts):
        copies.append(
            pltpu.make_async_copy(pack.at[:, first:last], held.at[:, to : to + last - first], sems.at[k])
        )
        copies[-1].start()
    return copies


def fetch_named(pack, named, sems, at):
    first = PLANE_NAMED_AT
    copies = [
        pltpu.make_async_copy(pack.at[:, first + k * LANES : first + (k + 1) * LANES], named.at[k], sems.at[at + k])
        for k in range(2)
    ]
    for copy in copies:
        copy.start()
    return copies


def chain_position(named, level, blocks):
    quarters = [
        named.at[a][pl.ds(2 * level + k, blocks, stride=BLOCK), :] for k in range(2) for a in range(2)
    ]
    return jnp.concatenate(quarters, axis=1).astype(jnp.int32) + (2 ** (level + 1) - 1) * LANES


def find_places(named, level, places):
    chain = chain_position(named, level, BLOCKS)
    if level == 0:
        block = lax.broadcasted_iota(jnp.int32, (BLOCKS, REACH), 0)
        places[...] = chain + jnp.where((chain < 3 * LANES) & (block < 16), 7 * LANES, 9 * LANES)
    else:
        places[...] = chain + 9 * LANES


def fetch_parts(parts, level, held, sems):
    first, last = LEVEL_AT[level]
    less = 0 if level < 3 else CUT
    copies, at = [], 0
    for k, part in enumerate(parts):
        count = part.shape[0]
        copies.append(
            pltpu.make_async_copy(part.at[:, first - less : last - less], held.at[pl.ds(at, count), :], sems.at[k])
        )
        copies[-1].start()
        at += count
    return copies


def path_solve(level, read, held, place, wide, total):
    diag_at, off_at = DIAG_AT[level] - LEVEL_AT[level][0], OFF_AT[level] - LEVEL_AT[level][0]
    for n in range(SPECIES):

        def write(at, value, n=n):
            wide[n, at : at + 64, :] = jnp.broadcast_to(value, (64, LANES))

        matvec(held, diag_at, 1, 2**level, functools.partial(read, n), write, OWN)
    names, lanes = small(rows_iota(PATH, 0)), small(rows_iota(LANES, 0))
    total[...] = jnp.zeros_like(total)

    def slot(d, carry):
        where = place[pl.ds(d, 1), :]
        hit = names == small(jnp.right_shift(where, 7))
        right = lane_one_hot(where, lanes)
        rows = block_rows(d)
        left = []
        for n in range(SPECIES):
            solved = jnp.concatenate([wide[n, rows, :]] * (REACH // LANES), axis=1)
            update = jnp.sum(held[rows, off_at : off_at + REACH] * solved, axis=0, keepdims=True)
            left += [pick(hit, part) for part in split(update)]
        total[...] += lax.dot_general(
            jnp.concatenate(left, axis=0), right, (((1,), (1,)), ((), ())), preferred_element_type=jnp.float32
        )
        return carry

    lax.fori_loop(0, SLOTS, slot, 0, unroll=8)


def path_update(level, before, total, path, ahead):
    count = 2 ** (level + 1)
    for n in range(SPECIES):
        at = 2 * n * PATH
        path[n * PATH : (n + 1) * PATH, :] = before[n * PATH : (n + 1) * PATH, :] - (
            total[at : at + PATH, :] + total[at + PATH : at + 2 * PATH, :]
        )
        if ahead is not None:
            ahead[n * count : (n + 1) * count, :] = path[n * PATH + count : n * PATH + 2 * count, :]


def path_first(*refs):
    parts = refs[: PARTS[0]]
    here, path, ahead, r0, places, held, named, turned, wide, total, sems = refs[PARTS[0] :]
    leaf, b = here[0], here[1]
    copies = fetch_parts(parts, 0, held, sems)
    path[...] = jnp.zeros((SPECIES * PATH, LANES), jnp.float32)
    lane = lax.broadcasted_iota(jnp.int32, (BLOCK, LANES), 1)
    row = lax.broadcasted_iota(jnp.int32, (BLOCK, LANES), 0)
    stands = []
    for core in (0, 1):
        for ahead_by in (0, 6, 2, 4):
            slot = jnp.bitwise_and(b + ahead_by, 7) ^ core
            stands.append(jnp.where(lane == row + slot * BLOCK, 1.0, 0.0).astype(jnp.bfloat16))
    order = jnp.concatenate(stands, axis=0)
    for copy in copies:
        copy.wait()
    flipped = jnp.transpose(held[:, RHS_AT : RHS_AT + 256])
    total_rows = None
    for _ in range(3):
        piece = flipped.astype(jnp.bfloat16)
        flipped = flipped - piece.astype(jnp.float32)
        rows = jnp.dot(piece, order, preferred_element_type=jnp.float32)
        total_rows = rows if total_rows is None else total_rows + rows
    turned[...] = total_rows
    for n in range(SPECIES):
        r0[n : n + 1, :] = turned[pl.ds(b * SPECIES + n, 1), :]
        for level in range(1, 6):
            at = n * PATH + 2**level + jnp.bitwise_and(leaf, 2**level - 1)
            path[pl.ds(at, 1), :] = turned[pl.ds(level * 32 + b * SPECIES + n, 1), :]
    for k in range(2):
        named[k] = held[:, NAMED_AT + k * LANES : NAMED_AT + (k + 1) * LANES]
    for level in range(5):
        places[level] = chain_position(named, level, SLOTS) + LANES
    path_solve(0, lambda n, c: r0[n : n + 1, :], held, places.at[0], wide, total)
    path_update(0, path, total, path, ahead)


def path_next(level, *refs):
    parts = refs[: PARTS[level]]
    places, summed, before, path, ahead, held, wide, total, sems = refs[PARTS[level] :]
    copies = fetch_parts(parts, level, held, sems)
    count = 2**level
    for copy in copies:
        copy.wait()
    path_solve(
        level, lambda n, c: summed[n * count + c : n * count + c + 1, :], held, places.at[level], wide, total
    )
    path_update(level, before, total, path, ahead)


def path_last(*refs):
    parts, (place, places, r0, r1, r2, r3, summed, before, keep, send, t2, t3, t4, path, *scratch) = (
        refs[: PARTS[4]], refs[PARTS[4] :]
    )
    path_next(4, *parts, places, summed, before, path, None, *scratch)
    x = place[0]
    even = 1.0 - (x & 1).astype(jnp.float32)
    for n in range(SPECIES):
        slot = n ^ x
        slot = slot ^ (slot >> 1)
        value = jnp.zeros((8, LANES), jnp.float32)
        row = lax.broadcasted_iota(jnp.int32, (8, LANES), 0)
        value = jnp.where(row == x, r0[n : n + 1, :], value)
        for k in range(2):
            value = jnp.where(row == 4 + 2 * (x >> 1) + k, r1[2 * n + k : 2 * n + k + 1, :] * even, value)
        for to, low in ((keep, 0), (send, 2)):

            @pl.when((slot >= low) & (slot < low + 2))
            def _(n=n, slot=slot, value=value, to=to, low=low):
                to[slot - low, 0:32, :] = path[n * PATH + 32 : (n + 1) * PATH, :]
                to[slot - low, 32:40, :] = value

    t2[...] = r2[pl.ds(x * 4, 4), :]
    t3[...] = r3[pl.ds(pl.multiple_of(x * 8, 8), 8), :]
    t4[...] = summed[pl.ds(pl.multiple_of(x * 16, 16), 16), :]


def high_cuts(level):
    columns = COUNT[level] * LANES
    return [
        (PLANE_DIAG_AT[level], PLANE_DIAG_AT[level] + columns, 0),
        (PLANE_OFF_AT[level], PLANE_OFF_AT[level] + REACH, columns),
    ]


def top(pack, summed, partial, held, wide, sems):
    pieces = 8
    size = ROWS // pieces

    def piece(k):
        rows = pl.ds(pl.multiple_of(k * size, size), size)
        columns = pl.ds(PLANE_DIAG_AT[5], COUNT[5] * LANES)
        return rows, pltpu.make_async_copy(pack.at[rows, columns], held.at[rows, :], sems.at[k])

    for k in range(pieces):
        piece(k)[1].start()
    partial[...] = jnp.zeros((COUNT[5], LANES), jnp.float32)

    @pl.loop(0, pieces)
    def _(k):
        rows, copy = piece(k)
        copy.wait()

        def write(at, value):
            wide[...] = jnp.broadcast_to(value, (size, LANES))

        matvec(held.at[rows, :], 0, 1, COUNT[5], lambda c: summed[c : c + 1, :], write, size)

        def write_row(c, value):
            partial[pl.ds(c, 1), :] = partial[pl.ds(c, 1), :] + value

        for c in range(COUNT[5]):
            term = held[rows, c * LANES : (c + 1) * LANES] * wide[...]
            write_row(c, jnp.sum(term, axis=0, keepdims=True))


def backward_high(level, pack, residual, *rest):
    above = rest[: 5 - level]
    partial, held, wide, chain, named, places, sems = rest[5 - level :]
    columns = COUNT[level] * LANES
    named_copies = fetch_named(pack, named, sems, 6)
    copies = fetch(pack, held, sems, high_cuts(level)[::-1])
    for k, value in enumerate(above):
        chain[FIRST[5 - k] : FIRST[5 - k] + COUNT[5 - k], :] = value[...]
    for copy in named_copies:
        copy.wait()
    find_places(named, level, places)
    copies[0].wait()
    couple(held, columns, chain, places, FIRST[level + 1], wide, BLOCKS)
    copies[1].wait()

    def write(at, value):
        wide[pl.ds(at, 64), :] = wide[pl.ds(at, 64), :] + value

    matvec(held, 0, 1, COUNT[level], lambda c: residual[c : c + 1, :], write)

    def write_row(c, value):
        partial[pl.ds(c, 1), :] = value

    matvec_transposed(held, 0, 1, COUNT[level], wide, write_row)


def backward_low(pack, r01, r2, s5, s4, s3, out, held, wide, chain, named, places, sems):
    named_copies = fetch_named(pack, named, sems, 6)
    cuts = []
    for level in (2, 1, 0):
        diag_at, off_at = PLANE_DIAG_AT[level], PLANE_OFF_AT[level]
        cuts.append((off_at, off_at + REACH, 896 + REACH * level))
        cuts.append((diag_at, diag_at + LANES * 2**level, LANES * (2**level - 1)))
    copies = fetch(pack, held, sems, cuts)
    for level, value in ((5, s5), (4, s4), (3, s3)):
        chain[FIRST[level] : FIRST[level] + COUNT[level], :] = value[...]
    chain[0:16, :] = jnp.zeros((16, LANES), jnp.float32)
    for copy in named_copies:
        copy.wait()
    for k, level in enumerate((2, 1, 0)):
        find_places(named, level, places)
        copies[2 * k].wait()
        couple(held, 896 + REACH * level, chain, places, 8, wide, BLOCKS)

        def write(at, value):
            wide[pl.ds(at, 64), :] = wide[pl.ds(at, 64), :] + value

        def read(c, level=level):
            return r2[c : c + 1, :] if level == 2 else r01[4 * level + c : 4 * level + c + 1, :]

        copies[2 * k + 1].wait()
        matvec(held, LANES * (2**level - 1), 4 >> level, 1 << level, read, write)

        def write_row(c, value, first=FIRST[level]):
            chain[first + c : first + c + 1, :] = value

        matvec_transposed(held, LANES * (2**level - 1), 4 >> level, 1 << level, wide, write_row)
    out[...] = chain[0:16, :]


def call(body, outs, scratch, args, far=1, scalar=(), sems=8):
    vmem = pl.BlockSpec(memory_space=pltpu.VMEM)
    smem = pl.BlockSpec(memory_space=pltpu.SMEM)
    hbm = pl.BlockSpec(memory_space=pltpu.HBM)
    specs = [hbm if k < far else smem if k in scalar else vmem for k in range(len(args))]
    return pl.pallas_call(
        body,
        out_shape=outs,
        in_specs=specs,
        out_specs=jax.tree.map(lambda _: vmem, outs),
        scratch_shapes=scratch + [pltpu.SemaphoreType.DMA((sems,))],
        compiler_params=pltpu.CompilerParams(vmem_limit_bytes=(52 if far == 1 else 6) * MIB),
        cost_estimate=pl.CostEstimate(flops=2**29, bytes_accessed=2**20, transcendentals=0),
    )(*args)


def shape(*dims, kind=jnp.float32):
    return jax.ShapeDtypeStruct(dims, kind)


def moved(value, axis, to):
    size = lax.axis_size(axis)
    return lax.ppermute(value, axis, [(i, to(i)) for i in range(size)])


def near_x(i):
    return 3 - i


def far_z(i):
    return (i + 5) % 8 if i % 2 else (i + 3) % 8


def sum_leaf(value, first, last):
    steps = [("x", lambda i: i ^ 1), ("x", near_x), ("z", lambda i: i ^ 1)]
    if last < 5:
        steps.append(("z", lambda i: i ^ 2))
    else:
        steps.append(("z", lambda i: (i + 1) % 8 if i % 2 else (i + 7) % 8))
        steps.append(("z", far_z))
    for axis, to in steps[first:last]:
        value = value + moved(value, axis, to)
    return value


def local(rhs, diag_inverse, off_diagonal, rows_index):
    f32 = jnp.float32
    x, z = lax.axis_index("x"), lax.axis_index("z")
    leaf = z * 4 + x
    hbm, vmem = pl.BlockSpec(memory_space=pltpu.HBM), pl.BlockSpec(memory_space=pltpu.VMEM)
    pack, first, second = pl.pallas_call(
        pack_all,
        out_shape=(shape(BLOCK, WHOLE), shape(BLOCK, CUT), shape(BLOCK, GROUP - CUT)),
        in_specs=[vmem, vmem, hbm, hbm],
        out_specs=(vmem,) * 3,
        scratch_shapes=[pltpu.SemaphoreType.DMA((16,))],
        compiler_params=pltpu.CompilerParams(vmem_limit_bytes=56 * MIB),
    )(jnp.transpose(rhs, (0, 2, 1)), rows_index, diag_inverse, off_diagonal)
    pack = lax.all_gather(pack, PLANE, axis=0, tiled=True)

    def other_core(parts):
        return parts + tuple(moved(part, "blk", lambda i: i ^ 1) for part in parts)

    def this_core(own):
        return (own,) + tuple(moved(own, "blk", lambda i, hop=hop: (i + hop) % SLOTS) for hop in (2, 6, 4))

    first = other_core(this_core(first))
    second = this_core(lax.optimization_barrier((second, first[-1]))[0])

    def path_scratch(level, *more):
        return [
            pltpu.VMEM((OWN, LEVEL_AT[level][1] - LEVEL_AT[level][0]), f32),
            *more,
            pltpu.VMEM((SPECIES, OWN, LANES), f32),
            pltpu.VMEM((SPECIES * 2 * PATH, LANES), f32),
        ]

    here = jnp.stack([leaf, lax.axis_index("blk")]).astype(jnp.int32)
    path, ahead, r0, places = call(
        path_first,
        (
            shape(SPECIES * PATH, LANES), shape(SPECIES * 2, LANES), shape(SPECIES, LANES),
            shape(5, SLOTS, REACH, kind=jnp.int32),
        ),
        path_scratch(0, pltpu.VMEM((2, OWN, LANES), f32), pltpu.VMEM((256, LANES), f32)),
        (*first, here),
        far=PARTS[0],
        scalar=(PARTS[0],),
        sems=PARTS[0],
    )
    waiting = [r0, sum_leaf(ahead, 0, 1)]
    for level in (1, 2, 3):
        path, ahead = call(
            functools.partial(path_next, level),
            (shape(SPECIES * PATH, LANES), shape(SPECIES * 2 ** (level + 1), LANES)),
            path_scratch(level),
            (*(first if level < 3 else second), places, waiting[level], path),
            far=PARTS[level],
            sems=PARTS[level],
        )
        if level == 2:
            second = other_core(lax.optimization_barrier((*second, ahead))[:4])
        waiting.append(sum_leaf(ahead, 0, level + 1))
    keep, send, r2, r3, r4 = call(
        path_last,
        (shape(2, 40, LANES), shape(2, 40, LANES), shape(4, LANES), shape(8, LANES), shape(16, LANES)),
        [pltpu.VMEM((SPECIES * PATH, LANES), f32)] + path_scratch(4),
        (*second, x.astype(jnp.int32).reshape(1), places, *waiting, path),
        far=PARTS[4],
        scalar=(PARTS[4],),
        sems=PARTS[4],
    )
    keep = keep + moved(send, "x", near_x)
    turned = keep[0] + moved(keep[1], "x", lambda i: i ^ 1)
    r5 = sum_leaf(turned[0:32], 2, 5)

    wide, chain = pltpu.VMEM((ROWS, LANES), f32), pltpu.VMEM((SPACE, LANES), f32)
    named, places = pltpu.VMEM((2, ROWS, LANES), f32), pltpu.VMEM((BLOCKS, REACH), jnp.int32)
    partial = call(top, shape(32, LANES), [pltpu.VMEM((ROWS, 32 * LANES), f32), pltpu.VMEM((ROWS // 8, LANES), f32)], (pack, r5))
    known = [sum_leaf(partial, 2, 5)]
    for level, from_rows in ((4, r4), (3, r3)):
        count = COUNT[level]
        partial = call(
            functools.partial(backward_high, level),
            shape(count, LANES),
            [pltpu.VMEM((ROWS, count * LANES + REACH), f32), wide, chain, named, places],
            (pack, from_rows, *known),
        )
        known.append(sum_leaf(partial, 2, level))
    last = call(
        backward_low,
        shape(16, LANES),
        [pltpu.VMEM((ROWS, 896 + 3 * REACH), f32), wide, chain, named, places],
        (pack, turned[32:40], r2, *known),
    )
    pieces = [last[0:4], last[8:12], last[12:16]]
    for level in (3, 4, 5):
        place = jnp.remainder(z, 2 ** (level - 2)) * 4
        pieces.append(lax.dynamic_slice_in_dim(known[5 - level], place, 4, 0))
    out = jnp.stack(pieces).reshape(6, BLOCKS, BLOCK)
    out = lax.all_to_all(jnp.transpose(out, (1, 0, 2)), PLANE, 0, 0)
    return jnp.transpose(out.reshape(SPECIES, SLOTS, 6, BLOCK), (2, 1, 0, 3)).reshape(6, BLOCKS, BLOCK)


def solution(mesh):
    cut = Mesh(mesh.devices.reshape(8, 4, 8), ("z", "x", "blk"))
    rows = ("z", "x", "blk")
    placed = (P(None, None, rows), P(rows, None), P(None, rows, None), P(None, rows, None))
    return jax.shard_map(
        local, mesh=cut, in_specs=placed, out_specs=P(None, None, rows), check_vma=False
    )
```
